32 devices in a mesh: group: 2 (over x), blk: 16 (over z, y, core).
Axes of the slice: x: 2, y: 2, z: 4, core: 2. Of those that a mesh axis runs over, the one named last changes fastest.
Arguments:
- traces: bfloat16 [128, 3, 2, 1200], P(('group', 'blk')), may hold values from -180 to 180, as said below
- assign: int32 [128], P(('group', 'blk')), may hold values from 0 to 3, as said below
- matching: int32 [16, 2], P('blk'), may hold values from 0 to 1, as said below
Outputs:
- between: bfloat16 [128, 4, 3, 3, 401], P(('group', 'blk'))
- within: bfloat16 [128, 4, 3, 3, 401], P(('group', 'blk'))
The draws below stay inside these ranges and needn't reach their ends.
Inputs may be any that keep to these rules, and one draw needn't show every extreme that they name: traces are finite records. `assign`: each aligned block of 4 entries, one device's stations, is a permutation of 0 to 3. `matching`: each row b is one round r_b, 0 to 1, of a round-robin plan with a bye round 0: group g is paired with g XOR r_b.
All inputs are finite; a program needn't handle non-finite values.
Results may differ from the reference program's by a relative error of at most 0.0082.
Values may be sent and summed in bfloat16 or wider, within the bound.
No kernel may reach another device: no remote copies, remote signals or barrier semaphores. Data moves between devices by JAX's collectives and lax.ppermute only.
A program may use at most 64 MiB of HBM per device.

```python
import math
import jax
import jax.numpy as jnp
from jax import lax

STA_DEV = 4
WIN = 2
NSAMP = 1200
PLEN = 1536
NF = 768
HALF = 200
LAGS = 401
GROUPS = 2
BLOCKS = 16
STATIONS = 128
N_BLK = 16


def draw_traces(key, part):
    noise_key = jax.random.fold_in(key, 11)
    scale_key = jax.random.fold_in(key, 13)
    noise_values = jnp.clip(jax.random.normal(noise_key, (STATIONS, 3, WIN, NSAMP), jnp.float32), -6.0, 6.0)
    log_scales = jax.random.uniform(scale_key, (STATIONS, 3, WIN, 1), jnp.float32, 0.0, math.log(10.0))
    return (noise_values * jnp.exp(log_scales)).astype(jnp.bfloat16)


def permute_block(block_key):
    return jax.random.permutation(block_key, STA_DEV)


def draw_assign(key, part):
    block_keys = jax.random.split(jax.random.fold_in(key, 23), STATIONS // STA_DEV)
    return jax.vmap(permute_block)(block_keys).reshape(-1).astype(jnp.int32)


def draw_matching(key, part):
    rounds = jax.random.randint(jax.random.fold_in(key, 37), (BLOCKS, 1), 0, GROUPS).astype(jnp.int32)
    players = jnp.arange(GROUPS, dtype=jnp.int32)[None, :]
    return jnp.bitwise_xor(players, rounds).astype(jnp.int32)


def setup_inputs(seed: int = 0) -> dict:
    splits = jax.random.split(jax.random.key(seed), 4)
    traces = draw_traces(jax.random.fold_in(splits[3], 71), 0)
    assign = draw_assign(jax.random.fold_in(splits[3], 71), 0)
    matching = draw_matching(jax.random.fold_in(splits[3], 71), 0)
    return {"traces": traces, "assign": assign, "matching": matching}


EPSILON = 1e-05

def forward_table():
    sample_ids = jnp.arange(NSAMP, dtype=jnp.int32)[:, None]
    bin_ids = jnp.arange(1, NF + 1, dtype=jnp.int32)[None, :]
    phases = (sample_ids * bin_ids % PLEN).astype(jnp.float32) * (2.0 * math.pi / PLEN)
    return jnp.concatenate([jnp.cos(phases), -jnp.sin(phases)], axis=1).astype(jnp.bfloat16)

def inverse_table():
    bin_ids = jnp.arange(1, NF + 1, dtype=jnp.int32)[:, None]
    lag_ids = jnp.arange(LAGS, dtype=jnp.int32)[None, :] - HALF
    phases = (bin_ids * lag_ids % PLEN).astype(jnp.float32) * (2.0 * math.pi / PLEN)
    return jnp.concatenate([jnp.cos(phases), -jnp.sin(phases)], axis=0).astype(jnp.bfloat16)

def correlate(local_spec, remote_spec, inverse):
    left = local_spec.astype(jnp.float32)
    right = remote_spec.astype(jnp.float32)
    left_re, left_im = (left[..., :NF], left[..., NF:])
    right_re, right_im = (right[..., :NF], right[..., NF:])

    def outer_sum(first_part, second_part):
        return jnp.einsum('acwk,bdwk->abcdk', first_part, second_part)
    real_part = outer_sum(left_re, right_re) + outer_sum(left_im, right_im)
    imag_part = outer_sum(left_re, right_im) - outer_sum(left_im, right_re)
    stacked = jnp.concatenate([real_part, imag_part], axis=-1).astype(jnp.bfloat16)
    lag_scale = 2.0 / (PLEN * math.sqrt(NSAMP * WIN))
    lag_values = jnp.dot(stacked.reshape(-1, 2 * NF), inverse, preferred_element_type=jnp.float32) * lag_scale
    return lag_values.astype(jnp.bfloat16).reshape(STA_DEV, STA_DEV, 3, 3, LAGS)

def reference(traces, assign, matching):
    device_total = STATIONS // STA_DEV
    row_ids = jnp.arange(STATIONS, dtype=jnp.int32)
    block_base = row_ids // STA_DEV * STA_DEV
    source_rows = jnp.zeros((STATIONS,), jnp.int32).at[block_base + assign].set(row_ids)
    ordered = traces[source_rows]
    values = ordered.astype(jnp.float32)
    energy = lax.optimization_barrier(jnp.mean(values * values, axis=-1, keepdims=True))
    normal = (values * lax.rsqrt(energy + EPSILON)).astype(jnp.bfloat16)
    forward = forward_table()
    inverse = inverse_table()
    spectra = jnp.dot(normal.reshape(-1, NSAMP), forward, preferred_element_type=jnp.float32)
    spectra = spectra.astype(jnp.bfloat16).reshape(device_total, STA_DEV, 3, WIN, PLEN)
    device_ids = jnp.arange(device_total, dtype=jnp.int32)
    group_ids = device_ids // N_BLK
    blk_ids = device_ids % N_BLK
    partner = matching[blk_ids, group_ids] * N_BLK + blk_ids
    neighbour = group_ids * N_BLK + (blk_ids - 1) % N_BLK

    def per_device(device):
        local_spec = spectra[device]
        return (correlate(local_spec, spectra[partner[device]], inverse), correlate(local_spec, spectra[neighbour[device]], inverse))
    between, within = lax.map(per_device, device_ids)
    return (between.reshape(STATIONS, STA_DEV, 3, 3, LAGS), within.reshape(STATIONS, STA_DEV, 3, 3, LAGS))
```

```python
import functools
import math

import jax
import jax.numpy as jnp
import ml_dtypes
import numpy as np
from jax import lax
from jax.experimental import pallas as pl
from jax.experimental.pallas import tpu as pltpu
from jax.sharding import PartitionSpec as P

STA = 4
COMP = 3
WIN = 2
NSAMP = 1200
PLEN = 1536
NF = 768
HALF = 200
LAGS = 401
ROWS = 16

EPSILON = 1e-05
LAG_SCALE = 2.0 / (PLEN * math.sqrt(NSAMP * WIN))


def forward_table():
    phases = np.arange(NSAMP)[:, None] * np.arange(1, NF + 1)[None, :] % PLEN * (2.0 * math.pi / PLEN)
    return np.concatenate([np.cos(phases), -np.sin(phases)], axis=1).astype(ml_dtypes.bfloat16)


def inverse_table():
    lags = np.arange(LAGS) - HALF
    phases = np.arange(1, NF + 1)[:, None] * lags[None, :] % PLEN * (2.0 * math.pi / PLEN)
    return np.concatenate([np.cos(phases), -np.sin(phases)], axis=0).astype(ml_dtypes.bfloat16)


def spectra_of(rows, forward):
    values = rows.astype(jnp.float32)
    energy = jnp.sum(values * values, axis=-1, keepdims=True) * (1.0 / NSAMP)
    normal = (values * lax.rsqrt(energy + EPSILON)).astype(jnp.bfloat16)
    result = jnp.dot(normal, forward, preferred_element_type=jnp.float32)
    return result.astype(jnp.bfloat16).astype(jnp.float32)


def own_kernel(rows_ref, forward_ref, spectra_ref):
    spectra_ref[...] = spectra_of(rows_ref[...], forward_ref[...])


def pair_kernel(rows_ref, left_ref, forward_ref, inverse_ref, out_ref, cross_ref):
    right = spectra_of(rows_ref[...], forward_ref[...])
    right_re = [right[w * ROWS : (w + 1) * ROWS, :NF] for w in range(WIN)]
    right_im = [right[w * ROWS : (w + 1) * ROWS, NF:] for w in range(WIN)]
    for a in range(STA):
        for i in range(COMP):
            real = jnp.zeros((ROWS, NF), jnp.float32)
            imag = jnp.zeros((ROWS, NF), jnp.float32)
            for w in range(WIN):
                row = w * ROWS + i * STA + a
                left_re = left_ref[row : row + 1, :NF]
                left_im = left_ref[row : row + 1, NF:]
                real += left_re * right_re[w] + left_im * right_im[w]
                imag += left_re * right_im[w] - left_im * right_re[w]
            base = (a * COMP + i) * ROWS
            cross_ref[base : base + ROWS, :NF] = real.astype(jnp.bfloat16)
            cross_ref[base : base + ROWS, NF:] = imag.astype(jnp.bfloat16)
    lags = jnp.dot(cross_ref[...], inverse_ref[...], preferred_element_type=jnp.float32) * LAG_SCALE
    for a in range(STA):
        for i in range(COMP):
            for j in range(COMP):
                row = (a * COMP + i) * ROWS + j * STA
                out_ref[a, i, j] = lags[row : row + STA].astype(jnp.bfloat16)


def in_vmem():
    return pl.BlockSpec(memory_space=pltpu.VMEM)


def own_spectra(rows, forward):
    return pl.pallas_call(
        own_kernel,
        out_shape=jax.ShapeDtypeStruct((WIN * ROWS, 2 * NF), jnp.float32),
        in_specs=[in_vmem()] * 2,
        out_specs=in_vmem(),
        compiler_params=pltpu.CompilerParams(vmem_limit_bytes=24 * 2**20),
        cost_estimate=pl.CostEstimate(flops=2 * 32 * NSAMP * 2 * NF, bytes_accessed=4_000_000, transcendentals=0),
    )(rows, forward)


def correlate(rows, left, forward, inverse):
    out = pl.pallas_call(
        pair_kernel,
        out_shape=jax.ShapeDtypeStruct((STA, COMP, COMP, STA, LAGS), jnp.bfloat16),
        in_specs=[in_vmem()] * 4,
        out_specs=in_vmem(),
        scratch_shapes=[pltpu.VMEM((STA * COMP * ROWS, 2 * NF), jnp.bfloat16)],
        compiler_params=pltpu.CompilerParams(vmem_limit_bytes=24 * 2**20),
        cost_estimate=pl.CostEstimate(flops=600_000_000, bytes_accessed=6_000_000, transcendentals=0),
    )(rows, left, forward, inverse)
    return out.transpose(0, 3, 1, 2, 4)


def shards(groups, blocks, traces, assign, matching):
    forward = jnp.asarray(forward_table())
    inverse = jnp.asarray(inverse_table())
    onehot = (assign[None, :] == jnp.arange(STA, dtype=jnp.int32)[:, None]).astype(jnp.bfloat16)
    ordered = jnp.einsum("sr,rcwt->wcst", onehot, traces, preferred_element_type=jnp.float32).astype(jnp.bfloat16)
    rows = jnp.pad(ordered.reshape(WIN, COMP * STA, NSAMP), ((0, 0), (0, ROWS - COMP * STA), (0, 0)))
    rows = rows.reshape(WIN * ROWS, NSAMP)
    beside = lax.ppermute(rows, "blk", [((i - 1) % blocks, i) for i in range(blocks)])
    remote = rows
    step = 1
    while step < groups:
        other = lax.ppermute(remote, "group", [(g ^ step, g) for g in range(groups)])
        remote = jnp.where((matching[0, 0] & step) != 0, other, remote)
        step *= 2
    left = own_spectra(rows, forward)
    between = correlate(remote, left, forward, inverse)
    within = correlate(beside, left, forward, inverse)
    return (between, within)


def solution(mesh):
    placed = (P(("group", "blk"), None, None, None), P(("group", "blk")), P("blk", None))
    return jax.shard_map(
        functools.partial(shards, mesh.shape["group"], mesh.shape["blk"]),
        mesh=mesh,
        in_specs=placed,
        out_specs=(
            P(("group", "blk"), None, None, None, None),
            P(("group", "blk"), None, None, None, None),
        ),
        check_vma=False,
    )
```

```python
import functools
import math

import jax
import jax.numpy as jnp
import ml_dtypes
import numpy as np
from jax import lax
from jax.experimental import pallas as pl
from jax.experimental.pallas import tpu as pltpu
from jax.sharding import PartitionSpec as P

STA = 4
COMP = 3
WIN = 2
NSAMP = 1200
PLEN = 1536
FOLD = PLEN // 2
NF = 768
QUARTER = NF // 2
HALF = 200
LAGS = 401
STEP = COMP * STA
LONG = 1280

EPSILON = 1e-05
LAG_SCALE = 2.0 / (PLEN * math.sqrt(NSAMP * WIN))

EVEN_BINS = np.arange(2, NF + 1, 2)
ODD_BINS = np.arange(1, NF + 1, 2)


def turned(ids_a, ids_b):
    phases = ids_a[:, None] * ids_b[None, :] % PLEN * (2.0 * math.pi / PLEN)
    return np.cos(phases), np.sin(phases)


def forward_table(bins):
    cosine, sine = turned(np.arange(FOLD), bins)
    return np.concatenate([cosine, -sine], axis=1).astype(ml_dtypes.bfloat16)


def inverse_table():
    lags = np.arange(LAGS) - HALF
    parts = []
    for bins in (EVEN_BINS, ODD_BINS):
        cosine, sine = turned(bins, lags)
        parts += [cosine, -sine]
    return np.concatenate(parts, axis=0).astype(ml_dtypes.bfloat16)


def spectra_of(rows, even_ref, odd_ref):
    values = rows.astype(jnp.float32)
    energy = jnp.sum(values * values, axis=-1, keepdims=True) * (1.0 / NSAMP)
    normal = values * lax.rsqrt(energy + EPSILON)
    early = normal[:, :FOLD]
    late = jnp.concatenate(
        [normal[:, FOLD:], jnp.zeros((rows.shape[0], PLEN - rows.shape[1]), jnp.float32)], axis=1
    )
    total = (early + late).astype(jnp.bfloat16)
    change = (early - late).astype(jnp.bfloat16)
    even = jnp.dot(total, even_ref[...], preferred_element_type=jnp.float32)
    odd = jnp.dot(change, odd_ref[...], preferred_element_type=jnp.float32)
    result = jnp.concatenate([even, odd], axis=1)
    return result.astype(jnp.bfloat16).astype(jnp.float32)


def cross_and_back(right, left_ref, inverse_ref, out_ref, cross_ref):
    first = lax.broadcasted_iota(jnp.int32, (2 * STEP, QUARTER), 0) < STEP
    for h in range(2):
        parts = []
        for begin in (h * NF, h * NF + QUARTER):
            for w in range(WIN):
                part = right[w * STEP : (w + 1) * STEP, begin : begin + QUARTER]
                parts.append(jnp.concatenate([part, part], axis=0))
        right_re, right_im = parts[:WIN], parts[WIN:]
        re, im = h * NF, h * NF + QUARTER
        for pair in range(STEP // 2):
            real = imag = None
            for w in range(WIN):
                rows = []
                for q in (2 * pair, 2 * pair + 1):
                    rows.append(w * STEP + q % COMP * STA + q // COMP)
                left_re = jnp.where(first, left_ref[rows[0] : rows[0] + 1, re : re + QUARTER], left_ref[rows[1] : rows[1] + 1, re : re + QUARTER])
                left_im = jnp.where(first, left_ref[rows[0] : rows[0] + 1, im : im + QUARTER], left_ref[rows[1] : rows[1] + 1, im : im + QUARTER])
                more_real = left_re * right_re[w] + left_im * right_im[w]
                more_imag = left_re * right_im[w] - left_im * right_re[w]
                real = more_real if real is None else real + more_real
                imag = more_imag if imag is None else imag + more_imag
            base = pair * 2 * STEP
            cross_ref[base : base + 2 * STEP, re : re + QUARTER] = real.astype(jnp.bfloat16)
            cross_ref[base : base + 2 * STEP, im : im + QUARTER] = imag.astype(jnp.bfloat16)
    lags = jnp.dot(cross_ref[...], inverse_ref[...], preferred_element_type=jnp.float32) * LAG_SCALE
    for a in range(STA):
        for i in range(COMP):
            for j in range(COMP):
                row = (a * COMP + i) * STEP + j * STA
                out_ref[a, i, j] = lags[row : row + STA].astype(jnp.bfloat16)


def order_kernel(traces_ref, assign_ref, long_ref, rows_ref, held, order, sems):
    fetch = pltpu.make_async_copy(traces_ref, held, sems.at[0])
    fetch_order = pltpu.make_async_copy(assign_ref, order, sems.at[1])
    fetch.start()
    fetch_order.start()
    fetch_order.wait()
    count = WIN * STEP
    row = lax.broadcasted_iota(jnp.int32, (count, count), 0)
    col = lax.broadcasted_iota(jnp.int32, (count, count), 1)
    target = col % WIN * STEP + col // WIN % COMP * STA
    for r in range(STA):
        target += jnp.where(col // (COMP * WIN) == r, order[0:1, r : r + 1], 0)
    move = (row == target).astype(jnp.float32).astype(jnp.bfloat16)
    fetch.wait()
    records = held[...].astype(jnp.float32).reshape(count, NSAMP).astype(jnp.bfloat16)
    placed = jnp.dot(move, records, preferred_element_type=jnp.float32).astype(jnp.bfloat16)
    rows_ref[...] = placed
    long_ref[...] = jnp.concatenate([placed, jnp.zeros((count, long_ref.shape[1] - NSAMP), jnp.bfloat16)], axis=1)


def own_kernel(rows_ref, even_ref, odd_ref, left_ref):
    left_ref[...] = spectra_of(rows_ref[...], even_ref, odd_ref)


def between_kernel(bit, rows_ref, left_ref, matching_ref, even_ref, odd_ref, inverse_ref, out_ref, cross_ref):
    other = spectra_of(rows_ref[...], even_ref, odd_ref)
    away = (matching_ref[:, 0:1] & bit) != 0
    right = jnp.where(away, other, left_ref[...])
    cross_and_back(right, left_ref, inverse_ref, out_ref, cross_ref)


def within_kernel(rows_ref, left_ref, even_ref, odd_ref, inverse_ref, between_ref, out_ref, between_out_ref, cross_ref, sem):
    leave = pltpu.make_async_copy(between_ref, between_out_ref, sem)
    leave.start()
    right = spectra_of(rows_ref[...], even_ref, odd_ref)
    cross_and_back(right, left_ref, inverse_ref, out_ref, cross_ref)
    leave.wait()


def in_vmem():
    return pl.BlockSpec(memory_space=pltpu.VMEM)


def in_hbm():
    return pl.BlockSpec(memory_space=pltpu.HBM)


OUT = jax.ShapeDtypeStruct((STA, COMP, COMP, STA, LAGS), jnp.bfloat16)
CROSS = pltpu.VMEM((STA * COMP * STEP, 2 * NF), jnp.bfloat16)


def params():
    return pltpu.CompilerParams(vmem_limit_bytes=24 * 2**20)


def order_rows(traces, assign):
    return pl.pallas_call(
        order_kernel,
        out_shape=[
            jax.ShapeDtypeStruct((WIN * STEP, LONG), jnp.bfloat16),
            jax.ShapeDtypeStruct((WIN * STEP, NSAMP), jnp.bfloat16),
        ],
        in_specs=[in_hbm(), in_hbm()],
        out_specs=[in_vmem(), in_vmem()],
        scratch_shapes=[
            pltpu.VMEM((STA, COMP, WIN, NSAMP), jnp.bfloat16),
            pltpu.VMEM((1, STA), jnp.int32),
            pltpu.SemaphoreType.DMA((2,)),
        ],
        compiler_params=params(),
        cost_estimate=pl.CostEstimate(flops=8_000_000_000, bytes_accessed=20_000_000, transcendentals=0),
    )(
        pltpu.with_memory_space_constraint(traces, pltpu.HBM),
        pltpu.with_memory_space_constraint(assign.reshape(1, STA), pltpu.HBM),
    )


def own_spectra(rows, even, odd):
    return pl.pallas_call(
        own_kernel,
        out_shape=jax.ShapeDtypeStruct((WIN * STEP, 2 * NF), jnp.float32),
        in_specs=[in_vmem()] * 3,
        out_specs=in_vmem(),
        compiler_params=params(),
        cost_estimate=pl.CostEstimate(flops=0, bytes_accessed=1000, transcendentals=0),
    )(rows, even, odd)


def correlate_between(bit, rows, left, matching, even, odd, inverse):
    return pl.pallas_call(
        functools.partial(between_kernel, bit),
        out_shape=OUT,
        in_specs=[in_vmem()] * 6,
        out_specs=in_vmem(),
        scratch_shapes=[CROSS],
        compiler_params=params(),
        cost_estimate=pl.CostEstimate(flops=0, bytes_accessed=1000, transcendentals=0),
    )(rows, left, matching, even, odd, inverse)


def correlate_within(rows, left, even, odd, inverse, between):
    return pl.pallas_call(
        within_kernel,
        out_shape=[OUT, OUT],
        in_specs=[in_vmem()] * 6,
        out_specs=[in_vmem(), pl.BlockSpec(memory_space=pl.ANY)],
        scratch_shapes=[CROSS, pltpu.SemaphoreType.DMA],
        compiler_params=params(),
        cost_estimate=pl.CostEstimate(flops=0, bytes_accessed=1000, transcendentals=0),
    )(rows, left, even, odd, inverse, between)


def shards(groups, blocks, traces, assign, matching):
    even = jnp.asarray(forward_table(EVEN_BINS))
    odd = jnp.asarray(forward_table(ODD_BINS))
    inverse = jnp.asarray(inverse_table())
    long_rows, rows = order_rows(traces, assign)
    beside = lax.ppermute(long_rows, "blk", [((i - 1) % blocks, i) for i in range(blocks)])
    remote = rows
    bit = 1
    while True:
        other = lax.ppermute(remote, "group", [(g ^ bit, g) for g in range(groups)])
        if bit * 2 >= groups:
            break
        remote = jnp.where((matching[0, 0] & bit) != 0, other, remote)
        bit *= 2
    left = own_spectra(rows, even, odd)
    between = correlate_between(bit, other, left, matching, even, odd, inverse)
    within, between = correlate_within(beside, left, even, odd, inverse, between)
    return (between.transpose(0, 3, 1, 2, 4), within.transpose(0, 3, 1, 2, 4))


def solution(mesh):
    placed = (P(("group", "blk"), None, None, None), P(("group", "blk")), P("blk", None))
    return jax.shard_map(
        functools.partial(shards, mesh.shape["group"], mesh.shape["blk"]),
        mesh=mesh,
        in_specs=placed,
        out_specs=(
            P(("group", "blk"), None, None, None, None),
            P(("group", "blk"), None, None, None, None),
        ),
        check_vma=False,
    )
```

```python
import functools
import math

import jax
import jax.numpy as jnp
import ml_dtypes
import numpy as np
from jax import lax
from jax.experimental import pallas as pl
from jax.experimental.pallas import tpu as pltpu
from jax.sharding import PartitionSpec as P

STA = 4
COMP = 3
WIN = 2
NSAMP = 1200
PLEN = 1536
NF = 768
QUARTER = PLEN // 4
HALF = 200
LAGS = 401
STEP = COMP * STA
LONG = 1280

EPSILON = 1e-05
LAG_SCALE = 2.0 / (PLEN * math.sqrt(NSAMP * WIN))

EVEN_BINS = np.concatenate([np.arange(4, NF + 1, 4), np.arange(2, NF + 1, 4)])
ODD_BINS = np.arange(1, PLEN, 4)


def turned(ids_a, ids_b):
    phases = ids_a[:, None] * ids_b[None, :] % PLEN * (2.0 * math.pi / PLEN)
    return np.cos(phases), np.sin(phases)


def forward_table(bins):
    cosine, sine = turned(np.arange(QUARTER), bins)
    return np.concatenate([cosine, -sine], axis=1).astype(ml_dtypes.bfloat16)


def inverse_table():
    lags = np.arange(LAGS) - HALF
    parts = []
    for bins in (EVEN_BINS, ODD_BINS):
        cosine, sine = turned(bins, lags)
        parts += [cosine, -sine]
    return np.concatenate(parts, axis=0).astype(ml_dtypes.bfloat16)


def through(first, second, table_ref):
    parts = []
    for values in (first, second):
        high = values.astype(jnp.bfloat16)
        parts += [high, (values - high.astype(jnp.float32)).astype(jnp.bfloat16)]
    count = first.shape[0]
    result = jnp.dot(jnp.concatenate(parts, axis=0), table_ref[...], preferred_element_type=jnp.float32)
    blocks = [result[n * count : (n + 1) * count] for n in range(4)]
    return blocks[0] + blocks[1], blocks[2] + blocks[3]


def once(values):
    return values.astype(jnp.bfloat16).astype(jnp.float32)


def spectra_of(rows, even_ref, odd_ref):
    normal = rows.astype(jnp.float32)
    count = rows.shape[0]
    rest = jnp.zeros((count, PLEN - rows.shape[1]), jnp.float32)
    quarters = [normal[:, n * QUARTER : (n + 1) * QUARTER] for n in range(3)]
    quarters.append(jnp.concatenate([normal[:, 3 * QUARTER :], rest], axis=1))
    sums = (quarters[0] + quarters[2], quarters[1] + quarters[3])
    total, change = through(sums[0] + sums[1], sums[0] - sums[1], even_ref)
    of_total = lax.broadcasted_iota(jnp.int32, (count, QUARTER), 1) < QUARTER // 2
    even = [jnp.where(of_total, total[:, half], change[:, half]) for half in (slice(0, QUARTER), slice(QUARTER, NF))]
    ahead, behind = through(quarters[0] - quarters[2], quarters[1] - quarters[3], odd_ref)
    odd = [ahead[:, :QUARTER] + behind[:, QUARTER:], ahead[:, QUARTER:] - behind[:, :QUARTER]]
    return [once(part) for part in even + odd]


def doubled(part, window):
    rows = part[window * STEP : (window + 1) * STEP]
    return jnp.concatenate([rows, rows], axis=0)


def cross_and_back(right, left_ref, inverse_ref, out_ref, cross_ref):
    middle = lax.broadcasted_iota(jnp.int32, (8, QUARTER), 0) < STEP - 8

    def left_rows(window, pair, begin):
        picked = []
        for q in (2 * pair, 2 * pair + 1):
            row = window * STEP + q % COMP * STA + q // COMP
            picked.append(jnp.broadcast_to(left_ref[row : row + 1, begin : begin + QUARTER], (8, QUARTER)))
        return jnp.concatenate([picked[0], jnp.where(middle, picked[0], picked[1]), picked[1]], axis=0)

    for h in range(2):
        re, im = h * NF, h * NF + QUARTER
        right_re = [doubled(right[2 * h], w) for w in range(WIN)]
        right_im = [doubled(right[2 * h + 1], w) for w in range(WIN)]
        for pair in range(STEP // 2):
            real, imag = 0.0, 0.0
            for w in range(WIN):
                left_re, left_im = left_rows(w, pair, re), left_rows(w, pair, im)
                real += left_re * right_re[w] + left_im * right_im[w]
                imag += left_re * right_im[w] - left_im * right_re[w]
            rows = slice(pair * 2 * STEP, (pair + 1) * 2 * STEP)
            cross_ref[rows, re : re + QUARTER] = real.astype(jnp.bfloat16)
            cross_ref[rows, im : im + QUARTER] = imag.astype(jnp.bfloat16)
    lags = jnp.dot(cross_ref[...], inverse_ref[...], preferred_element_type=jnp.float32) * LAG_SCALE
    out_ref[...] = lags.astype(jnp.bfloat16).reshape(out_ref.shape)


def order_kernel(traces_ref, assign_ref, rows_ref, held, order, placed, sems):
    fetch_order = pltpu.make_async_copy(assign_ref, order, sems.at[STA])
    fetch_order.start()
    fetches = [pltpu.make_async_copy(traces_ref.at[r], held.at[r], sems.at[r]) for r in range(STA)]
    for fetch in fetches:
        fetch.start()
    last = LONG - 128
    placed[:, last:] = jnp.zeros((WIN * STEP, 128), jnp.float32)
    fetch_order.wait()
    for r in range(STA):
        fetches[r].wait()
        place = order[r]
        for j in range(COMP):
            both = held[r, j].astype(jnp.float32)
            for w in range(WIN):
                placed[pl.ds(w * STEP + j * STA + place, 1), :NSAMP] = both[w : w + 1]
    values = placed[...]
    energy = jnp.sum(values * values, axis=-1, keepdims=True) * (1.0 / NSAMP)
    rows_ref[...] = (values * lax.rsqrt(energy + EPSILON)).astype(jnp.bfloat16)


def short_kernel(long_ref, rows_ref):
    rows_ref[...] = long_ref[:, :NSAMP]


def own_kernel(rows_ref, even_ref, odd_ref, left_ref):
    for n, part in enumerate(spectra_of(rows_ref[...], even_ref, odd_ref)):
        left_ref[:, n * QUARTER : (n + 1) * QUARTER] = part


def between_kernel(bit, rows_ref, left_ref, matching_ref, even_ref, odd_ref, inverse_ref, out_ref, cross_ref):
    other = spectra_of(rows_ref[...], even_ref, odd_ref)
    away = (matching_ref[:, 0:1] & bit) != 0
    right = [jnp.where(away, part, left_ref[:, n * QUARTER : (n + 1) * QUARTER]) for n, part in enumerate(other)]
    cross_and_back(right, left_ref, inverse_ref, out_ref, cross_ref)


def within_kernel(
    rows_ref, left_ref, even_ref, odd_ref, inverse_ref, between_ref, out_ref, between_out_ref, cross_ref, sem
):
    right = spectra_of(rows_ref[...], even_ref, odd_ref)
    leave = pltpu.make_async_copy(between_ref, between_out_ref, sem)
    leave.start()
    cross_and_back(right, left_ref, inverse_ref, out_ref, cross_ref)
    leave.wait()


def in_vmem():
    return pl.BlockSpec(memory_space=pltpu.VMEM)


def in_hbm():
    return pl.BlockSpec(memory_space=pltpu.HBM)


OUT = jax.ShapeDtypeStruct((STA, COMP, COMP, STA, LAGS), jnp.bfloat16)
CROSS = pltpu.VMEM((STA * COMP * STEP, 2 * NF), jnp.bfloat16)


def params():
    return pltpu.CompilerParams(vmem_limit_bytes=24 * 2**20)


def order_rows(traces, assign):
    return pl.pallas_call(
        order_kernel,
        out_shape=jax.ShapeDtypeStruct((WIN * STEP, LONG), jnp.bfloat16),
        in_specs=[in_hbm(), in_hbm()],
        out_specs=in_vmem(),
        scratch_shapes=[
            pltpu.VMEM((STA, COMP, WIN, NSAMP), jnp.bfloat16),
            pltpu.SMEM((STA,), jnp.int32),
            pltpu.VMEM((WIN * STEP, LONG), jnp.float32),
            pltpu.SemaphoreType.DMA((STA + 1,)),
        ],
        compiler_params=params(),
        cost_estimate=pl.CostEstimate(flops=0, bytes_accessed=100_000, transcendentals=0),
    )(pltpu.with_memory_space_constraint(traces, pltpu.HBM), pltpu.with_memory_space_constraint(assign, pltpu.HBM))


def short_rows(long_rows):
    return pl.pallas_call(
        short_kernel,
        out_shape=jax.ShapeDtypeStruct((WIN * STEP, NSAMP), jnp.bfloat16),
        in_specs=[in_vmem()],
        out_specs=in_vmem(),
        compiler_params=params(),
        cost_estimate=pl.CostEstimate(flops=8_000_000_000, bytes_accessed=20_000_000, transcendentals=0),
    )(long_rows)


def own_spectra(rows, even, odd):
    return pl.pallas_call(
        own_kernel,
        out_shape=jax.ShapeDtypeStruct((WIN * STEP, 2 * NF), jnp.float32),
        in_specs=[in_vmem()] * 3,
        out_specs=in_vmem(),
        compiler_params=params(),
        cost_estimate=pl.CostEstimate(flops=0, bytes_accessed=1000, transcendentals=0),
    )(rows, even, odd)


def correlate_between(bit, rows, left, matching, even, odd, inverse):
    return pl.pallas_call(
        functools.partial(between_kernel, bit),
        out_shape=OUT,
        in_specs=[in_vmem()] * 6,
        out_specs=in_vmem(),
        scratch_shapes=[CROSS],
        compiler_params=params(),
        cost_estimate=pl.CostEstimate(flops=0, bytes_accessed=1000, transcendentals=0),
    )(rows, left, matching, even, odd, inverse)


def correlate_within(rows, left, even, odd, inverse, between):
    return pl.pallas_call(
        within_kernel,
        out_shape=[OUT, OUT],
        in_specs=[in_vmem()] * 6,
        out_specs=[in_vmem(), pl.BlockSpec(memory_space=pl.ANY)],
        scratch_shapes=[CROSS, pltpu.SemaphoreType.DMA],
        compiler_params=params(),
        cost_estimate=pl.CostEstimate(flops=0, bytes_accessed=1000, transcendentals=0),
    )(rows, left, even, odd, inverse, between)


def shards(groups, blocks, traces, assign, matching):
    even = jnp.asarray(forward_table(EVEN_BINS))
    odd = jnp.asarray(forward_table(ODD_BINS))
    inverse = jnp.asarray(inverse_table())
    long_rows = order_rows(traces, assign)
    beside = lax.ppermute(long_rows, "blk", [((i - 1) % blocks, i) for i in range(blocks)])
    rows = short_rows(long_rows)
    remote = rows
    bit = 1
    while True:
        other = lax.ppermute(remote, "group", [(g ^ bit, g) for g in range(groups)])
        if bit * 2 >= groups:
            break
        remote = jnp.where((matching[0, 0] & bit) != 0, other, remote)
        bit *= 2
    left = own_spectra(rows, even, odd)
    between = correlate_between(bit, other, left, matching, even, odd, inverse)
    within, between = correlate_within(beside, left, even, odd, inverse, between)
    return (between.transpose(0, 3, 1, 2, 4), within.transpose(0, 3, 1, 2, 4))


def solution(mesh):
    placed = (P(("group", "blk"), None, None, None), P(("group", "blk")), P("blk", None))
    return jax.shard_map(
        functools.partial(shards, mesh.shape["group"], mesh.shape["blk"]),
        mesh=mesh,
        in_specs=placed,
        out_specs=(
            P(("group", "blk"), None, None, None, None),
            P(("group", "blk"), None, None, None, None),
        ),
        check_vma=False,
    )
```

```python
import functools
import math

import jax
import jax.numpy as jnp
import ml_dtypes
import numpy as np
from jax import lax
from jax.experimental import pallas as pl
from jax.experimental.pallas import tpu as pltpu
from jax.sharding import PartitionSpec as P

STA = 4
COMP = 3
WIN = 2
NSAMP = 1200
PLEN = 1536
NF = 768
QUARTER = PLEN // 4
HALF = 200
LAGS = 401
STEP = COMP * STA
LONG = 1280

EPSILON = 1e-05
LAG_SCALE = 2.0 / (PLEN * math.sqrt(NSAMP * WIN))

EVEN_BINS = np.concatenate([np.arange(4, NF + 1, 4), np.arange(2, NF + 1, 4)])
ODD_BINS = np.arange(1, PLEN, 4)


def turned(ids_a, ids_b):
    phases = ids_a[:, None] * ids_b[None, :] % PLEN * (2.0 * math.pi / PLEN)
    return np.cos(phases), np.sin(phases)


def forward_table(bins):
    cosine, sine = turned(np.arange(QUARTER), bins)
    return np.concatenate([cosine, -sine], axis=1).astype(ml_dtypes.bfloat16)


def inverse_table():
    lags = np.arange(LAGS) - HALF
    parts = []
    for bins in (EVEN_BINS, ODD_BINS):
        cosine, sine = turned(bins, lags)
        parts += [cosine, -sine]
    return np.concatenate(parts, axis=0).astype(ml_dtypes.bfloat16)


def through(first, second, table_ref):
    parts = []
    for values in (first, second):
        high = values.astype(jnp.bfloat16)
        parts += [high, (values - high.astype(jnp.float32)).astype(jnp.bfloat16)]
    count = first.shape[0]
    result = jnp.dot(jnp.concatenate(parts, axis=0), table_ref[...], preferred_element_type=jnp.float32)
    blocks = [result[n * count : (n + 1) * count] for n in range(4)]
    return blocks[0] + blocks[1], blocks[2] + blocks[3]


def once(values):
    return values.astype(jnp.bfloat16).astype(jnp.float32)


def spectra_of(rows, even_ref, odd_ref):
    normal = rows.astype(jnp.float32)
    count = rows.shape[0]
    rest = jnp.zeros((count, PLEN - rows.shape[1]), jnp.float32)
    quarters = [normal[:, n * QUARTER : (n + 1) * QUARTER] for n in range(3)]
    quarters.append(jnp.concatenate([normal[:, 3 * QUARTER :], rest], axis=1))
    sums = (quarters[0] + quarters[2], quarters[1] + quarters[3])
    total, change = through(sums[0] + sums[1], sums[0] - sums[1], even_ref)
    of_total = lax.broadcasted_iota(jnp.int32, (count, QUARTER), 1) < QUARTER // 2
    even = [jnp.where(of_total, total[:, half], change[:, half]) for half in (slice(0, QUARTER), slice(QUARTER, NF))]
    ahead, behind = through(quarters[0] - quarters[2], quarters[1] - quarters[3], odd_ref)
    odd = [ahead[:, :QUARTER] + behind[:, QUARTER:], ahead[:, QUARTER:] - behind[:, :QUARTER]]
    return [once(part) for part in even + odd]


def doubled(part, window):
    rows = part[window * STEP : (window + 1) * STEP]
    return jnp.concatenate([rows, rows], axis=0)


def cross_and_back(right, left_ref, inverse_ref, out_ref, cross_ref):
    middle = lax.broadcasted_iota(jnp.int32, (8, QUARTER), 0) < STEP - 8

    def left_rows(window, pair, begin):
        picked = []
        for q in (2 * pair, 2 * pair + 1):
            row = window * STEP + q % COMP * STA + q // COMP
            picked.append(jnp.broadcast_to(left_ref[row : row + 1, begin : begin + QUARTER], (8, QUARTER)))
        return jnp.concatenate([picked[0], jnp.where(middle, picked[0], picked[1]), picked[1]], axis=0)

    for h in range(2):
        re, im = h * NF, h * NF + QUARTER
        right_re = [doubled(right[2 * h], w) for w in range(WIN)]
        right_im = [doubled(right[2 * h + 1], w) for w in range(WIN)]
        for pair in range(STEP // 2):
            real, imag = 0.0, 0.0
            for w in range(WIN):
                left_re, left_im = left_rows(w, pair, re), left_rows(w, pair, im)
                real += left_re * right_re[w] + left_im * right_im[w]
                imag += left_re * right_im[w] - left_im * right_re[w]
            rows = slice(pair * 2 * STEP, (pair + 1) * 2 * STEP)
            cross_ref[rows, re : re + QUARTER] = real.astype(jnp.bfloat16)
            cross_ref[rows, im : im + QUARTER] = imag.astype(jnp.bfloat16)
    lags = jnp.dot(cross_ref[...], inverse_ref[...], preferred_element_type=jnp.float32) * LAG_SCALE
    out_ref[...] = lags.astype(jnp.bfloat16).reshape(out_ref.shape)


def order_kernel(traces_ref, assign_ref, rows_ref, held, order, placed, sems):
    fetch_order = pltpu.make_async_copy(assign_ref, order, sems.at[STA])
    fetch_order.start()
    fetches = [pltpu.make_async_copy(traces_ref.at[r], held.at[r], sems.at[r]) for r in range(STA)]
    for fetch in fetches:
        fetch.start()
    last = LONG - 128
    placed[:, last:] = jnp.zeros((WIN * STEP, 128), jnp.float32)
    fetch_order.wait()
    for r in range(STA):
        fetches[r].wait()
        place = order[r]
        for j in range(COMP):
            both = held[r, j].astype(jnp.float32)
            for w in range(WIN):
                placed[pl.ds(w * STEP + j * STA + place, 1), :NSAMP] = both[w : w + 1]
    values = placed[...]
    energy = jnp.sum(values * values, axis=-1, keepdims=True) * (1.0 / NSAMP)
    rows_ref[...] = (values * lax.rsqrt(energy + EPSILON)).astype(jnp.bfloat16)


def short_kernel(long_ref, rows_ref):
    rows_ref[...] = long_ref[:, :NSAMP]


def own_kernel(rows_ref, even_ref, odd_ref, left_ref):
    for n, part in enumerate(spectra_of(rows_ref[...], even_ref, odd_ref)):
        left_ref[:, n * QUARTER : (n + 1) * QUARTER] = part


def between_kernel(bit, rows_ref, left_ref, matching_ref, even_ref, odd_ref, inverse_ref, out_ref, cross_ref):
    other = spectra_of(rows_ref[...], even_ref, odd_ref)
    away = (matching_ref[:, 0:1] & bit) != 0
    right = [jnp.where(away, part, left_ref[:, n * QUARTER : (n + 1) * QUARTER]) for n, part in enumerate(other)]
    cross_and_back(right, left_ref, inverse_ref, out_ref, cross_ref)


def within_kernel(rows_ref, left_ref, even_ref, odd_ref, inverse_ref, between_ref, out_ref, between_out_ref, cross_ref):
    right = spectra_of(rows_ref[...], even_ref, odd_ref)
    cross_and_back(right, left_ref, inverse_ref, out_ref, cross_ref)
    between_out_ref[...] = between_ref[...]


def in_vmem():
    return pl.BlockSpec(memory_space=pltpu.VMEM)


def in_hbm():
    return pl.BlockSpec(memory_space=pltpu.HBM)


OUT = jax.ShapeDtypeStruct((STA, COMP, COMP, STA, LAGS), jnp.bfloat16)
CROSS = pltpu.VMEM((STA * COMP * STEP, 2 * NF), jnp.bfloat16)


def params():
    return pltpu.CompilerParams(vmem_limit_bytes=24 * 2**20)


def order_rows(traces, assign):
    return pl.pallas_call(
        order_kernel,
        out_shape=jax.ShapeDtypeStruct((WIN * STEP, LONG), jnp.bfloat16),
        in_specs=[in_hbm(), in_hbm()],
        out_specs=in_vmem(),
        scratch_shapes=[
            pltpu.VMEM((STA, COMP, WIN, NSAMP), jnp.bfloat16),
            pltpu.SMEM((STA,), jnp.int32),
            pltpu.VMEM((WIN * STEP, LONG), jnp.float32),
            pltpu.SemaphoreType.DMA((STA + 1,)),
        ],
        compiler_params=params(),
        cost_estimate=pl.CostEstimate(flops=0, bytes_accessed=100_000, transcendentals=0),
    )(pltpu.with_memory_space_constraint(traces, pltpu.HBM), pltpu.with_memory_space_constraint(assign, pltpu.HBM))


def short_rows(long_rows):
    return pl.pallas_call(
        short_kernel,
        out_shape=jax.ShapeDtypeStruct((WIN * STEP, NSAMP), jnp.bfloat16),
        in_specs=[in_vmem()],
        out_specs=in_vmem(),
        compiler_params=params(),
        cost_estimate=pl.CostEstimate(flops=8_000_000_000, bytes_accessed=20_000_000, transcendentals=0),
    )(long_rows)


def own_spectra(rows, even, odd):
    return pl.pallas_call(
        own_kernel,
        out_shape=jax.ShapeDtypeStruct((WIN * STEP, 2 * NF), jnp.float32),
        in_specs=[in_vmem()] * 3,
        out_specs=in_vmem(),
        compiler_params=params(),
        cost_estimate=pl.CostEstimate(flops=0, bytes_accessed=1000, transcendentals=0),
    )(rows, even, odd)


def correlate_between(bit, rows, left, matching, even, odd, inverse):
    return pl.pallas_call(
        functools.partial(between_kernel, bit),
        out_shape=OUT,
        in_specs=[in_vmem()] * 6,
        out_specs=in_vmem(),
        scratch_shapes=[CROSS],
        compiler_params=params(),
        cost_estimate=pl.CostEstimate(flops=0, bytes_accessed=1000, transcendentals=0),
    )(rows, left, matching, even, odd, inverse)


def correlate_within(rows, left, even, odd, inverse, between):
    return pl.pallas_call(
        within_kernel,
        out_shape=[OUT, OUT],
        in_specs=[in_vmem()] * 6,
        out_specs=[in_vmem(), in_vmem()],
        scratch_shapes=[CROSS],
        compiler_params=params(),
        cost_estimate=pl.CostEstimate(flops=0, bytes_accessed=1000, transcendentals=0),
    )(rows, left, even, odd, inverse, between)


def shards(groups, blocks, traces, assign, matching):
    even = jnp.asarray(forward_table(EVEN_BINS))
    odd = jnp.asarray(forward_table(ODD_BINS))
    inverse = jnp.asarray(inverse_table())
    long_rows = order_rows(traces, assign)
    beside = lax.ppermute(long_rows, "blk", [((i - 1) % blocks, i) for i in range(blocks)])
    rows = short_rows(long_rows)
    remote = rows
    bit = 1
    while True:
        other = lax.ppermute(remote, "group", [(g ^ bit, g) for g in range(groups)])
        if bit * 2 >= groups:
            break
        remote = jnp.where((matching[0, 0] & bit) != 0, other, remote)
        bit *= 2
    left = own_spectra(rows, even, odd)
    between = correlate_between(bit, other, left, matching, even, odd, inverse)
    within, between = correlate_within(beside, left, even, odd, inverse, between)
    return (between.transpose(0, 3, 1, 2, 4), within.transpose(0, 3, 1, 2, 4))


def solution(mesh):
    placed = (P(("group", "blk"), None, None, None), P(("group", "blk")), P("blk", None))
    return jax.shard_map(
        functools.partial(shards, mesh.shape["group"], mesh.shape["blk"]),
        mesh=mesh,
        in_specs=placed,
        out_specs=(
            P(("group", "blk"), None, None, None, None),
            P(("group", "blk"), None, None, None, None),
        ),
        check_vma=False,
    )
```

```python
import functools
import math

import jax
import jax.numpy as jnp
import ml_dtypes
import numpy as np
from jax import lax
from jax.experimental import pallas as pl
from jax.experimental.pallas import tpu as pltpu
from jax.sharding import PartitionSpec as P

STA = 4
COMP = 3
WIN = 2
NSAMP = 1200
PLEN = 1536
NF = 768
QUARTER = PLEN // 4
HALF = 200
LAGS = 401
STEP = COMP * STA
LONG = 1280

EPSILON = 1e-05
LAG_SCALE = 2.0 / (PLEN * math.sqrt(NSAMP * WIN))

EVEN_BINS = np.concatenate([np.arange(4, NF + 1, 4), np.arange(2, NF + 1, 4)])
ODD_BINS = np.arange(1, PLEN, 4)


def turned(ids_a, ids_b):
    phases = ids_a[:, None] * ids_b[None, :] % PLEN * (2.0 * math.pi / PLEN)
    return np.cos(phases), np.sin(phases)


def forward_table(bins):
    cosine, sine = turned(np.arange(QUARTER), bins)
    return np.concatenate([cosine, -sine], axis=1).astype(ml_dtypes.bfloat16)


def inverse_table():
    lags = np.arange(LAGS) - HALF
    parts = []
    for bins in (EVEN_BINS, ODD_BINS):
        cosine, sine = turned(bins, lags)
        parts += [cosine, -sine]
    return np.concatenate(parts, axis=0).astype(ml_dtypes.bfloat16)


def through(first, second, table):
    parts = []
    for values in (first, second):
        high = values.astype(jnp.bfloat16)
        parts += [high, (values - high.astype(jnp.float32)).astype(jnp.bfloat16)]
    count = first.shape[0]
    result = jnp.dot(jnp.concatenate(parts, axis=0), table, preferred_element_type=jnp.float32)
    blocks = [result[n * count : (n + 1) * count] for n in range(4)]
    return blocks[0] + blocks[1], blocks[2] + blocks[3]


def once(values):
    return values.astype(jnp.bfloat16).astype(jnp.float32)


def spectra_of(rows, forward_ref):
    normal = rows.astype(jnp.float32)
    count = rows.shape[0]
    rest = jnp.zeros((count, PLEN - rows.shape[1]), jnp.float32)
    quarters = [normal[:, n * QUARTER : (n + 1) * QUARTER] for n in range(3)]
    quarters.append(jnp.concatenate([normal[:, 3 * QUARTER :], rest], axis=1))
    sums = (quarters[0] + quarters[2], quarters[1] + quarters[3])
    total, change = through(sums[0] + sums[1], sums[0] - sums[1], forward_ref[:QUARTER])
    of_total = lax.broadcasted_iota(jnp.int32, (count, QUARTER), 1) < QUARTER // 2
    even = [jnp.where(of_total, total[:, half], change[:, half]) for half in (slice(0, QUARTER), slice(QUARTER, NF))]
    ahead, behind = through(quarters[0] - quarters[2], quarters[1] - quarters[3], forward_ref[QUARTER:])
    odd = [ahead[:, :QUARTER] + behind[:, QUARTER:], ahead[:, QUARTER:] - behind[:, :QUARTER]]
    return [once(part) for part in even + odd]


def doubled(part, window):
    rows = part[window * STEP : (window + 1) * STEP]
    return jnp.concatenate([rows, rows], axis=0)


def cross_and_back(right, left_ref, inverse_ref, out_ref):
    middle = lax.broadcasted_iota(jnp.int32, (8, QUARTER), 0) < STEP - 8

    def left_rows(window, pair, begin):
        picked = []
        for q in (2 * pair, 2 * pair + 1):
            row = window * STEP + q % COMP * STA + q // COMP
            picked.append(jnp.broadcast_to(left_ref[row : row + 1, begin : begin + QUARTER], (8, QUARTER)))
        return jnp.concatenate([picked[0], jnp.where(middle, picked[0], picked[1]), picked[1]], axis=0)

    columns = []
    for h in range(2):
        re, im = h * NF, h * NF + QUARTER
        right_re = [doubled(right[2 * h], w) for w in range(WIN)]
        right_im = [doubled(right[2 * h + 1], w) for w in range(WIN)]
        reals, imags = [], []
        for pair in range(STEP // 2):
            real, imag = 0.0, 0.0
            for w in range(WIN):
                left_re, left_im = left_rows(w, pair, re), left_rows(w, pair, im)
                real += left_re * right_re[w] + left_im * right_im[w]
                imag += left_re * right_im[w] - left_im * right_re[w]
            reals.append(real.astype(jnp.bfloat16))
            imags.append(imag.astype(jnp.bfloat16))
        columns += [jnp.concatenate(reals, axis=0), jnp.concatenate(imags, axis=0)]
    cross = jnp.concatenate(columns, axis=1)
    lags = jnp.dot(cross, inverse_ref[...], preferred_element_type=jnp.float32) * LAG_SCALE
    out_ref[...] = lags.astype(jnp.bfloat16).reshape(out_ref.shape)


def order_kernel(traces_ref, assign_ref, rows_ref, held, order, placed, sems):
    fetch_order = pltpu.make_async_copy(assign_ref, order, sems.at[STA])
    fetch_order.start()
    fetches = [pltpu.make_async_copy(traces_ref.at[r], held.at[r], sems.at[r]) for r in range(STA)]
    for fetch in fetches:
        fetch.start()
    last = LONG - 128
    placed[:, last:] = jnp.zeros((WIN * STEP, 128), jnp.float32)
    fetch_order.wait()
    for r in range(STA):
        fetches[r].wait()
        place = order[r]
        for j in range(COMP):
            both = held[r, j].astype(jnp.float32)
            for w in range(WIN):
                placed[pl.ds(w * STEP + j * STA + place, 1), :NSAMP] = both[w : w + 1]
    values = placed[...]
    energy = jnp.sum(values * values, axis=-1, keepdims=True) * (1.0 / NSAMP)
    rows_ref[...] = (values * lax.rsqrt(energy + EPSILON)).astype(jnp.bfloat16)


def short_kernel(long_ref, rows_ref):
    rows_ref[...] = long_ref[:, :NSAMP]


def own_kernel(rows_ref, *refs):
    sources, (left_ref, *targets), sems = refs[:3], refs[3:7], refs[7]
    fetches = [pltpu.make_async_copy(sources[n], targets[n], sems.at[n]) for n in range(3)]
    for fetch in fetches:
        fetch.start()
    fetches[0].wait()
    for n, part in enumerate(spectra_of(rows_ref[...], targets[0])):
        left_ref[:, n * QUARTER : (n + 1) * QUARTER] = part
    fetches[1].wait()
    fetches[2].wait()


def between_kernel(bit, rows_ref, left_ref, plan_ref, forward_ref, inverse_ref, out_ref):
    other = spectra_of(rows_ref[...], forward_ref)
    away = (plan_ref[:, 0:1] & bit) != 0
    right = [jnp.where(away, part, left_ref[:, n * QUARTER : (n + 1) * QUARTER]) for n, part in enumerate(other)]
    cross_and_back(right, left_ref, inverse_ref, out_ref)


def within_kernel(rows_ref, left_ref, forward_ref, inverse_ref, between_ref, out_ref, between_out_ref):
    right = spectra_of(rows_ref[...], forward_ref)
    cross_and_back(right, left_ref, inverse_ref, out_ref)
    between_out_ref[...] = between_ref[...]


def in_vmem():
    return pl.BlockSpec(memory_space=pltpu.VMEM)


def in_hbm():
    return pl.BlockSpec(memory_space=pltpu.HBM)


OUT = jax.ShapeDtypeStruct((STA, COMP, COMP, STA, LAGS), jnp.bfloat16)


COST = pl.CostEstimate(flops=0, bytes_accessed=1000, transcendentals=0)


def params():
    return pltpu.CompilerParams(vmem_limit_bytes=24 * 2**20)


def order_rows(traces, assign):
    return pl.pallas_call(
        order_kernel,
        out_shape=jax.ShapeDtypeStruct((WIN * STEP, LONG), jnp.bfloat16),
        in_specs=[in_hbm(), in_hbm()],
        out_specs=in_vmem(),
        scratch_shapes=[
            pltpu.VMEM((STA, COMP, WIN, NSAMP), jnp.bfloat16),
            pltpu.SMEM((STA,), jnp.int32),
            pltpu.VMEM((WIN * STEP, LONG), jnp.float32),
            pltpu.SemaphoreType.DMA((STA + 1,)),
        ],
        compiler_params=params(),
        cost_estimate=COST,
    )(pltpu.with_memory_space_constraint(traces, pltpu.HBM), pltpu.with_memory_space_constraint(assign, pltpu.HBM))


def short_rows(long_rows):
    return pl.pallas_call(
        short_kernel,
        out_shape=jax.ShapeDtypeStruct((WIN * STEP, NSAMP), jnp.bfloat16),
        in_specs=[in_vmem()],
        out_specs=in_vmem(),
        compiler_params=params(),
        cost_estimate=COST,
    )(long_rows)


def own_spectra(rows, *arrays):
    return pl.pallas_call(
        own_kernel,
        out_shape=[jax.ShapeDtypeStruct((WIN * STEP, 2 * NF), jnp.float32)]
        + [jax.ShapeDtypeStruct(array.shape, array.dtype) for array in arrays],
        in_specs=[in_vmem()] + [in_hbm()] * 3,
        out_specs=[in_vmem()] * 4,
        scratch_shapes=[pltpu.SemaphoreType.DMA((3,))],
        compiler_params=params(),
        cost_estimate=COST,
    )(rows, *(pltpu.with_memory_space_constraint(array, pltpu.HBM) for array in arrays))


def correlate_between(bit, rows, left, plan, forward, inverse):
    return pl.pallas_call(
        functools.partial(between_kernel, bit),
        out_shape=OUT,
        in_specs=[in_vmem()] * 5,
        out_specs=in_vmem(),
        compiler_params=params(),
        cost_estimate=COST,
    )(rows, left, plan, forward, inverse)


def correlate_within(rows, left, forward, inverse, between):
    return pl.pallas_call(
        within_kernel,
        out_shape=[OUT, OUT],
        in_specs=[in_vmem()] * 5,
        out_specs=[in_vmem(), in_vmem()],
        compiler_params=params(),
        cost_estimate=COST,
    )(rows, left, forward, inverse, between)


def shards(groups, blocks, traces, assign, matching):
    forward = jnp.asarray(np.concatenate([forward_table(EVEN_BINS), forward_table(ODD_BINS)], axis=0))
    inverse = jnp.asarray(inverse_table())
    long_rows = order_rows(traces, assign)
    beside = lax.ppermute(long_rows, "blk", [((i - 1) % blocks, i) for i in range(blocks)])
    rows = short_rows(long_rows)
    remote = rows
    bit = 1
    while True:
        other = lax.ppermute(remote, "group", [(g ^ bit, g) for g in range(groups)])
        if bit * 2 >= groups:
            break
        remote = jnp.where((matching[0, 0] & bit) != 0, other, remote)
        bit *= 2
    left, forward, inverse, plan = own_spectra(long_rows, forward, inverse, matching)
    between = correlate_between(bit, other, left, plan, forward, inverse)
    within, between = correlate_within(beside, left, forward, inverse, between)
    return (between.transpose(0, 3, 1, 2, 4), within.transpose(0, 3, 1, 2, 4))


def solution(mesh):
    placed = (P(("group", "blk"), None, None, None), P(("group", "blk")), P("blk", None))
    return jax.shard_map(
        functools.partial(shards, mesh.shape["group"], mesh.shape["blk"]),
        mesh=mesh,
        in_specs=placed,
        out_specs=(
            P(("group", "blk"), None, None, None, None),
            P(("group", "blk"), None, None, None, None),
        ),
        check_vma=False,
    )
```

```python
import functools
import math

import jax
import jax.numpy as jnp
import ml_dtypes
import numpy as np
from jax import lax
from jax.experimental import pallas as pl
from jax.experimental.pallas import tpu as pltpu
from jax.sharding import PartitionSpec as P

STA = 4
COMP = 3
WIN = 2
NSAMP = 1200
PLEN = 1536
NF = 768
QUARTER = PLEN // 4
HALF = 200
LAGS = 401
STEP = COMP * STA
LONG = 1280

EPSILON = 1e-05
LAG_SCALE = 2.0 / (PLEN * math.sqrt(NSAMP * WIN))

EVEN_BINS = np.concatenate([np.arange(4, NF + 1, 4), np.arange(2, NF + 1, 4)])
ODD_BINS = np.arange(1, PLEN, 4)


def turned(ids_a, ids_b):
    phases = ids_a[:, None] * ids_b[None, :] % PLEN * (2.0 * math.pi / PLEN)
    return np.cos(phases), np.sin(phases)


def forward_table(bins):
    cosine, sine = turned(np.arange(QUARTER), bins)
    return np.concatenate([cosine, -sine], axis=1).astype(ml_dtypes.bfloat16)


def inverse_table():
    lags = np.arange(LAGS) - HALF
    parts = []
    for bins in (EVEN_BINS, ODD_BINS):
        cosine, sine = turned(bins, lags)
        parts += [cosine, -sine]
    return np.concatenate(parts, axis=0).astype(ml_dtypes.bfloat16)


def through(first, second, table):
    parts = []
    for values in (first, second):
        high = values.astype(jnp.bfloat16)
        parts += [high, (values - high.astype(jnp.float32)).astype(jnp.bfloat16)]
    count = first.shape[0]
    result = jnp.dot(jnp.concatenate(parts, axis=0), table, preferred_element_type=jnp.float32)
    blocks = [result[n * count : (n + 1) * count] for n in range(4)]
    return blocks[0] + blocks[1], blocks[2] + blocks[3]


def once(values):
    return values.astype(jnp.bfloat16).astype(jnp.float32)


def spectra_of(rows, forward_ref):
    normal = rows.astype(jnp.float32)
    count = rows.shape[0]
    rest = jnp.zeros((count, PLEN - rows.shape[1]), jnp.float32)
    quarters = [normal[:, n * QUARTER : (n + 1) * QUARTER] for n in range(3)]
    quarters.append(jnp.concatenate([normal[:, 3 * QUARTER :], rest], axis=1))
    sums = (quarters[0] + quarters[2], quarters[1] + quarters[3])
    total, change = through(sums[0] + sums[1], sums[0] - sums[1], forward_ref[:QUARTER])
    of_total = lax.broadcasted_iota(jnp.int32, (count, QUARTER), 1) < QUARTER // 2
    even = [jnp.where(of_total, total[:, half], change[:, half]) for half in (slice(0, QUARTER), slice(QUARTER, NF))]
    ahead, behind = through(quarters[0] - quarters[2], quarters[1] - quarters[3], forward_ref[QUARTER:])
    odd = [ahead[:, :QUARTER] + behind[:, QUARTER:], ahead[:, QUARTER:] - behind[:, :QUARTER]]
    return [once(part) for part in even + odd]


def doubled(part, window):
    rows = part[window * STEP : (window + 1) * STEP]
    return jnp.concatenate([rows, rows], axis=0)


def cross_and_back(right, left_ref, inverse_ref, out_ref):
    middle = lax.broadcasted_iota(jnp.int32, (8, QUARTER), 0) < STEP - 8

    def left_rows(window, pair, begin):
        picked = []
        for q in (2 * pair, 2 * pair + 1):
            row = window * STEP + q % COMP * STA + q // COMP
            picked.append(jnp.broadcast_to(left_ref[row : row + 1, begin : begin + QUARTER], (8, QUARTER)))
        return jnp.concatenate([picked[0], jnp.where(middle, picked[0], picked[1]), picked[1]], axis=0)

    columns = []
    for h in range(2):
        re, im = h * NF, h * NF + QUARTER
        right_re = [doubled(right[2 * h], w) for w in range(WIN)]
        right_im = [doubled(right[2 * h + 1], w) for w in range(WIN)]
        reals, imags = [], []
        for pair in range(STEP // 2):
            real, imag = 0.0, 0.0
            for w in range(WIN):
                left_re, left_im = left_rows(w, pair, re), left_rows(w, pair, im)
                real += left_re * right_re[w] + left_im * right_im[w]
                imag += left_re * right_im[w] - left_im * right_re[w]
            reals.append(real.astype(jnp.bfloat16))
            imags.append(imag.astype(jnp.bfloat16))
        columns += [jnp.concatenate(reals, axis=0), jnp.concatenate(imags, axis=0)]
    cross = jnp.concatenate(columns, axis=1)
    lags = jnp.dot(cross, inverse_ref[...], preferred_element_type=jnp.float32) * LAG_SCALE
    out_ref[...] = lags.astype(jnp.bfloat16).reshape(out_ref.shape)


def order_kernel(traces_ref, assign_ref, rows_ref, held, order, placed, sems):
    fetch_order = pltpu.make_async_copy(assign_ref, order, sems.at[STA])
    fetch_order.start()
    fetches = [pltpu.make_async_copy(traces_ref.at[r], held.at[r], sems.at[r]) for r in range(STA)]
    for fetch in fetches:
        fetch.start()
    last = LONG - 128
    placed[:, last:] = jnp.zeros((WIN * STEP, 128), jnp.float32)
    fetch_order.wait()
    for r in range(STA):
        fetches[r].wait()
        place = order[r]
        for j in range(COMP):
            both = held[r, j].astype(jnp.float32)
            for w in range(WIN):
                placed[pl.ds(w * STEP + j * STA + place, 1), :NSAMP] = both[w : w + 1]
    values = placed[...]
    energy = jnp.sum(values * values, axis=-1, keepdims=True) * (1.0 / NSAMP)
    rows_ref[...] = (values * lax.rsqrt(energy + EPSILON)).astype(jnp.bfloat16)


def short_kernel(long_ref, rows_ref):
    rows_ref[...] = long_ref[:, :NSAMP]


def own_kernel(rows_ref, *refs):
    sources, (left_ref, *targets), sems = refs[:3], refs[3:7], refs[7]
    fetches = [pltpu.make_async_copy(sources[n], targets[n], sems.at[n]) for n in range(3)]
    for fetch in fetches:
        fetch.start()
    fetches[0].wait()
    for n, part in enumerate(spectra_of(rows_ref[...], targets[0])):
        left_ref[:, n * QUARTER : (n + 1) * QUARTER] = part
    fetches[1].wait()
    fetches[2].wait()


def between_kernel(choose, rows_ref, left_ref, plan_ref, forward_ref, inverse_ref, out_ref):
    right = spectra_of(rows_ref[...], forward_ref)
    if choose:
        away = plan_ref[:, 0:1] != 0
        right = [jnp.where(away, part, left_ref[:, n * QUARTER : (n + 1) * QUARTER]) for n, part in enumerate(right)]
    cross_and_back(right, left_ref, inverse_ref, out_ref)


def within_kernel(rows_ref, left_ref, forward_ref, inverse_ref, between_ref, out_ref, between_out_ref):
    right = spectra_of(rows_ref[...], forward_ref)
    cross_and_back(right, left_ref, inverse_ref, out_ref)
    between_out_ref[...] = between_ref[...]


def in_vmem():
    return pl.BlockSpec(memory_space=pltpu.VMEM)


def in_hbm():
    return pl.BlockSpec(memory_space=pltpu.HBM)


OUT = jax.ShapeDtypeStruct((STA, COMP, COMP, STA, LAGS), jnp.bfloat16)


COST = pl.CostEstimate(flops=0, bytes_accessed=1000, transcendentals=0)


def params():
    return pltpu.CompilerParams(vmem_limit_bytes=24 * 2**20)


def order_rows(traces, assign):
    return pl.pallas_call(
        order_kernel,
        out_shape=jax.ShapeDtypeStruct((WIN * STEP, LONG), jnp.bfloat16),
        in_specs=[in_hbm(), in_hbm()],
        out_specs=in_vmem(),
        scratch_shapes=[
            pltpu.VMEM((STA, COMP, WIN, NSAMP), jnp.bfloat16),
            pltpu.SMEM((STA,), jnp.int32),
            pltpu.VMEM((WIN * STEP, LONG), jnp.float32),
            pltpu.SemaphoreType.DMA((STA + 1,)),
        ],
        compiler_params=params(),
        cost_estimate=COST,
    )(pltpu.with_memory_space_constraint(traces, pltpu.HBM), pltpu.with_memory_space_constraint(assign, pltpu.HBM))


def short_rows(long_rows):
    return pl.pallas_call(
        short_kernel,
        out_shape=jax.ShapeDtypeStruct((WIN * STEP, NSAMP), jnp.bfloat16),
        in_specs=[in_vmem()],
        out_specs=in_vmem(),
        compiler_params=params(),
        cost_estimate=COST,
    )(long_rows)


def own_spectra(rows, *arrays):
    return pl.pallas_call(
        own_kernel,
        out_shape=[jax.ShapeDtypeStruct((WIN * STEP, 2 * NF), jnp.float32)]
        + [jax.ShapeDtypeStruct(array.shape, array.dtype) for array in arrays],
        in_specs=[in_vmem()] + [in_hbm()] * 3,
        out_specs=[in_vmem()] * 4,
        scratch_shapes=[pltpu.SemaphoreType.DMA((3,))],
        compiler_params=params(),
        cost_estimate=COST,
    )(rows, *(pltpu.with_memory_space_constraint(array, pltpu.HBM) for array in arrays))


def correlate_between(choose, rows, left, plan, forward, inverse):
    return pl.pallas_call(
        functools.partial(between_kernel, choose),
        out_shape=OUT,
        in_specs=[in_vmem()] * 5,
        out_specs=in_vmem(),
        compiler_params=params(),
        cost_estimate=COST,
    )(rows, left, plan, forward, inverse)


def correlate_within(rows, left, forward, inverse, between):
    return pl.pallas_call(
        within_kernel,
        out_shape=[OUT, OUT],
        in_specs=[in_vmem()] * 5,
        out_specs=[in_vmem(), in_vmem()],
        compiler_params=params(),
        cost_estimate=COST,
    )(rows, left, forward, inverse, between)


def shards(groups, blocks, traces, assign, matching):
    forward = jnp.asarray(np.concatenate([forward_table(EVEN_BINS), forward_table(ODD_BINS)], axis=0))
    inverse = jnp.asarray(inverse_table())
    long_rows = order_rows(traces, assign)
    beside = lax.ppermute(long_rows, "blk", [((i - 1) % blocks, i) for i in range(blocks)])
    other = short_rows(long_rows)
    bits = [1 << n for n in range((groups - 1).bit_length())]
    for bit in bits:
        swapped = lax.ppermute(other, "group", [(g ^ bit, g) for g in range(groups)])
        other = swapped if groups == 2 else jnp.where((matching[0, 0] & bit) != 0, swapped, other)
    left, forward, inverse, plan = own_spectra(long_rows, forward, inverse, matching)
    between = correlate_between(groups == 2, other, left, plan, forward, inverse)
    within, between = correlate_within(beside, left, forward, inverse, between)
    return (between.transpose(0, 3, 1, 2, 4), within.transpose(0, 3, 1, 2, 4))


def solution(mesh):
    placed = (P(("group", "blk"), None, None, None), P(("group", "blk")), P("blk", None))
    return jax.shard_map(
        functools.partial(shards, mesh.shape["group"], mesh.shape["blk"]),
        mesh=mesh,
        in_specs=placed,
        out_specs=(
            P(("group", "blk"), None, None, None, None),
            P(("group", "blk"), None, None, None, None),
        ),
        check_vma=False,
    )
```

```python
import functools
import math

import jax
import jax.numpy as jnp
import ml_dtypes
import numpy as np
from jax import lax
from jax.experimental import pallas as pl
from jax.experimental.pallas import tpu as pltpu
from jax.sharding import PartitionSpec as P

STA = 4
COMP = 3
WIN = 2
NSAMP = 1200
PLEN = 1536
NF = 768
QUARTER = PLEN // 4
HALF = 200
LAGS = 401
STEP = COMP * STA
LONG = 1280

EPSILON = 1e-05
LAG_SCALE = 2.0 / (PLEN * math.sqrt(NSAMP * WIN))

EVEN_BINS = np.concatenate([np.arange(4, NF + 1, 4), np.arange(2, NF + 1, 4)])
ODD_BINS = np.arange(1, PLEN, 4)


def turned(ids_a, ids_b):
    phases = ids_a[:, None] * ids_b[None, :] % PLEN * (2.0 * math.pi / PLEN)
    return np.cos(phases), np.sin(phases)


def forward_table(bins):
    cosine, sine = turned(np.arange(QUARTER), bins)
    return np.concatenate([cosine, -sine], axis=1).astype(ml_dtypes.bfloat16)


def inverse_table():
    lags = np.arange(LAGS) - HALF
    parts = []
    for bins in (EVEN_BINS, ODD_BINS):
        cosine, sine = turned(bins, lags)
        parts += [cosine, -sine]
    return np.concatenate(parts, axis=0).astype(ml_dtypes.bfloat16)


def through(first, second, table):
    parts = []
    for values in (first, second):
        high = values.astype(jnp.bfloat16)
        parts += [high, (values - high.astype(jnp.float32)).astype(jnp.bfloat16)]
    count = first.shape[0]
    result = jnp.dot(jnp.concatenate(parts, axis=0), table, preferred_element_type=jnp.float32)
    blocks = [result[n * count : (n + 1) * count] for n in range(4)]
    return blocks[0] + blocks[1], blocks[2] + blocks[3]


def once(values):
    return values.astype(jnp.bfloat16).astype(jnp.float32)


def spectra_of(rows, forward_ref):
    normal = rows.astype(jnp.float32)
    count = rows.shape[0]
    rest = jnp.zeros((count, PLEN - rows.shape[1]), jnp.float32)
    quarters = [normal[:, n * QUARTER : (n + 1) * QUARTER] for n in range(3)]
    quarters.append(jnp.concatenate([normal[:, 3 * QUARTER :], rest], axis=1))
    sums = (quarters[0] + quarters[2], quarters[1] + quarters[3])
    total, change = through(sums[0] + sums[1], sums[0] - sums[1], forward_ref[:QUARTER])
    of_total = lax.broadcasted_iota(jnp.int32, (count, QUARTER), 1) < QUARTER // 2
    even = [jnp.where(of_total, total[:, half], change[:, half]) for half in (slice(0, QUARTER), slice(QUARTER, NF))]
    ahead, behind = through(quarters[0] - quarters[2], quarters[1] - quarters[3], forward_ref[QUARTER:])
    odd = [ahead[:, :QUARTER] + behind[:, QUARTER:], ahead[:, QUARTER:] - behind[:, :QUARTER]]
    return [once(part) for part in even + odd]


def doubled(part, window):
    rows = part[window * STEP : (window + 1) * STEP]
    return jnp.concatenate([rows, rows], axis=0)


def cross_and_back(right, left_ref, inverse_ref, out_ref):
    middle = lax.broadcasted_iota(jnp.int32, (8, QUARTER), 0) < STEP - 8

    def left_rows(window, pair, begin):
        picked = []
        for q in (2 * pair, 2 * pair + 1):
            row = window * STEP + q % COMP * STA + q // COMP
            picked.append(jnp.broadcast_to(left_ref[row : row + 1, begin : begin + QUARTER], (8, QUARTER)))
        return jnp.concatenate([picked[0], jnp.where(middle, picked[0], picked[1]), picked[1]], axis=0)

    columns = []
    for h in range(2):
        re, im = h * NF, h * NF + QUARTER
        right_re = [doubled(right[2 * h], w) for w in range(WIN)]
        right_im = [doubled(right[2 * h + 1], w) for w in range(WIN)]
        reals, imags = [], []
        for pair in range(STEP // 2):
            real, imag = 0.0, 0.0
            for w in range(WIN):
                left_re, left_im = left_rows(w, pair, re), left_rows(w, pair, im)
                real += left_re * right_re[w] + left_im * right_im[w]
                imag += left_re * right_im[w] - left_im * right_re[w]
            reals.append(real.astype(jnp.bfloat16))
            imags.append(imag.astype(jnp.bfloat16))
        columns += [jnp.concatenate(reals, axis=0), jnp.concatenate(imags, axis=0)]
    cross = jnp.concatenate(columns, axis=1)
    lags = jnp.dot(cross, inverse_ref[...], preferred_element_type=jnp.float32) * LAG_SCALE
    out_ref[...] = lags.astype(jnp.bfloat16).reshape(out_ref.shape)


def order_kernel(traces_ref, assign_ref, rows_ref, held, order, placed, sems):
    fetch_order = pltpu.make_async_copy(assign_ref, order, sems.at[STA])
    fetch_order.start()
    fetches = [pltpu.make_async_copy(traces_ref.at[r], held.at[r], sems.at[r]) for r in range(STA)]
    for fetch in fetches:
        fetch.start()
    last = LONG - 128
    placed[:, last:] = jnp.zeros((WIN * STEP, 128), jnp.float32)
    fetch_order.wait()
    for r in range(STA):
        fetches[r].wait()
        place = order[r]
        for j in range(COMP):
            both = held[r, j].astype(jnp.float32)
            for w in range(WIN):
                placed[pl.ds(w * STEP + j * STA + place, 1), :NSAMP] = both[w : w + 1]
    values = placed[...]
    energy = jnp.sum(values * values, axis=-1, keepdims=True) * (1.0 / NSAMP)
    rows_ref[...] = (values * lax.rsqrt(energy + EPSILON)).astype(jnp.bfloat16)


def short_kernel(long_ref, rows_ref):
    rows_ref[...] = long_ref[:, :NSAMP]


def own_kernel(rows_ref, *refs):
    sources, (left_ref, *targets), sems = refs[:3], refs[3:7], refs[7]
    fetches = [pltpu.make_async_copy(sources[n], targets[n], sems.at[n]) for n in range(3)]
    for fetch in fetches:
        fetch.start()
    fetches[0].wait()
    for n, part in enumerate(spectra_of(rows_ref[...], targets[0])):
        left_ref[:, n * QUARTER : (n + 1) * QUARTER] = part
    fetches[1].wait()
    fetches[2].wait()


def between_kernel(choose, rows_ref, left_ref, plan_ref, forward_ref, inverse_ref, out_ref, away_ref, sem):
    right = spectra_of(rows_ref[...], forward_ref)
    if choose:
        away = plan_ref[:, 0:1] != 0
        right = [jnp.where(away, part, left_ref[:, n * QUARTER : (n + 1) * QUARTER]) for n, part in enumerate(right)]
    cross_and_back(right, left_ref, inverse_ref, out_ref)

    @pl.when(lax.axis_index("blk") == 0)
    def _():
        leave = pltpu.make_async_copy(out_ref, away_ref, sem)
        leave.start()
        leave.wait()


def within_kernel(rows_ref, left_ref, forward_ref, inverse_ref, between_ref, early_ref, out_ref, between_out_ref, sem):
    del early_ref
    cross_and_back(spectra_of(rows_ref[...], forward_ref), left_ref, inverse_ref, out_ref)

    @pl.when(lax.axis_index("blk") != 0)
    def _():
        leave = pltpu.make_async_copy(between_ref, between_out_ref, sem)
        leave.start()
        leave.wait()


def in_vmem():
    return pl.BlockSpec(memory_space=pltpu.VMEM)


def in_hbm():
    return pl.BlockSpec(memory_space=pltpu.HBM)


OUT = jax.ShapeDtypeStruct((STA, COMP, COMP, STA, LAGS), jnp.bfloat16)


COST = pl.CostEstimate(flops=0, bytes_accessed=1000, transcendentals=0)


def params():
    return pltpu.CompilerParams(vmem_limit_bytes=24 * 2**20)


def order_rows(traces, assign):
    return pl.pallas_call(
        order_kernel,
        out_shape=jax.ShapeDtypeStruct((WIN * STEP, LONG), jnp.bfloat16),
        in_specs=[in_hbm(), in_hbm()],
        out_specs=in_vmem(),
        scratch_shapes=[
            pltpu.VMEM((STA, COMP, WIN, NSAMP), jnp.bfloat16),
            pltpu.SMEM((STA,), jnp.int32),
            pltpu.VMEM((WIN * STEP, LONG), jnp.float32),
            pltpu.SemaphoreType.DMA((STA + 1,)),
        ],
        compiler_params=params(),
        cost_estimate=COST,
    )(pltpu.with_memory_space_constraint(traces, pltpu.HBM), pltpu.with_memory_space_constraint(assign, pltpu.HBM))


def short_rows(long_rows):
    return pl.pallas_call(
        short_kernel,
        out_shape=jax.ShapeDtypeStruct((WIN * STEP, NSAMP), jnp.bfloat16),
        in_specs=[in_vmem()],
        out_specs=in_vmem(),
        compiler_params=params(),
        cost_estimate=COST,
    )(long_rows)


def own_spectra(rows, *arrays):
    return pl.pallas_call(
        own_kernel,
        out_shape=[jax.ShapeDtypeStruct((WIN * STEP, 2 * NF), jnp.float32)]
        + [jax.ShapeDtypeStruct(array.shape, array.dtype) for array in arrays],
        in_specs=[in_vmem()] + [in_hbm()] * 3,
        out_specs=[in_vmem()] * 4,
        scratch_shapes=[pltpu.SemaphoreType.DMA((3,))],
        compiler_params=params(),
        cost_estimate=COST,
    )(rows, *(pltpu.with_memory_space_constraint(array, pltpu.HBM) for array in arrays))


def anywhere():
    return pl.BlockSpec(memory_space=pl.ANY)


def correlate_between(choose, rows, left, plan, forward, inverse):
    return pl.pallas_call(
        functools.partial(between_kernel, choose),
        out_shape=[OUT, OUT],
        in_specs=[in_vmem()] * 5,
        out_specs=[in_vmem(), anywhere()],
        scratch_shapes=[pltpu.SemaphoreType.DMA],
        compiler_params=params(),
        cost_estimate=COST,
    )(rows, left, plan, forward, inverse)


def correlate_within(rows, left, forward, inverse, between, early):
    return pl.pallas_call(
        within_kernel,
        out_shape=[OUT, OUT],
        in_specs=[in_vmem()] * 5 + [anywhere()],
        out_specs=[in_vmem(), anywhere()],
        scratch_shapes=[pltpu.SemaphoreType.DMA],
        input_output_aliases={5: 1},
        compiler_params=params(),
        cost_estimate=COST,
    )(rows, left, forward, inverse, between, early)


def shards(groups, blocks, traces, assign, matching):
    forward = jnp.asarray(np.concatenate([forward_table(EVEN_BINS), forward_table(ODD_BINS)], axis=0))
    inverse = jnp.asarray(inverse_table())
    long_rows = order_rows(traces, assign)
    beside = lax.ppermute(long_rows, "blk", [((i - 1) % blocks, i) for i in range(blocks)])
    other = short_rows(long_rows)
    bits = [1 << n for n in range((groups - 1).bit_length())]
    for bit in bits:
        swapped = lax.ppermute(other, "group", [(g ^ bit, g) for g in range(groups)])
        other = swapped if groups == 2 else jnp.where((matching[0, 0] & bit) != 0, swapped, other)
    left, forward, inverse, plan = own_spectra(long_rows, forward, inverse, matching)
    between, early = correlate_between(groups == 2, other, left, plan, forward, inverse)
    within, between = correlate_within(beside, left, forward, inverse, between, early)
    return (between.transpose(0, 3, 1, 2, 4), within.transpose(0, 3, 1, 2, 4))


def solution(mesh):
    placed = (P(("group", "blk"), None, None, None), P(("group", "blk")), P("blk", None))
    return jax.shard_map(
        functools.partial(shards, mesh.shape["group"], mesh.shape["blk"]),
        mesh=mesh,
        in_specs=placed,
        out_specs=(
            P(("group", "blk"), None, None, None, None),
            P(("group", "blk"), None, None, None, None),
        ),
        check_vma=False,
    )
```

```python
import functools
import math

import jax
import jax.numpy as jnp
import ml_dtypes
import numpy as np
from jax import lax
from jax.experimental import pallas as pl
from jax.experimental.pallas import tpu as pltpu
from jax.sharding import PartitionSpec as P

STA = 4
COMP = 3
WIN = 2
NSAMP = 1200
PLEN = 1536
NF = 768
QUARTER = PLEN // 4
HALF = 200
LAGS = 401
STEP = COMP * STA
LONG = 1280

EPSILON = 1e-05
LAG_SCALE = 2.0 / (PLEN * math.sqrt(NSAMP * WIN))

EVEN_BINS = np.concatenate([np.arange(4, NF + 1, 4), np.arange(2, NF + 1, 4)])
ODD_BINS = np.arange(1, PLEN, 4)


def turned(ids_a, ids_b):
    phases = ids_a[:, None] * ids_b[None, :] % PLEN * (2.0 * math.pi / PLEN)
    return np.cos(phases), np.sin(phases)


def forward_table(bins):
    cosine, sine = turned(np.arange(QUARTER), bins)
    return np.concatenate([cosine, -sine], axis=1).astype(ml_dtypes.bfloat16)


def inverse_table():
    lags = np.arange(LAGS) - HALF
    parts = []
    for bins in (EVEN_BINS, ODD_BINS):
        cosine, sine = turned(bins, lags)
        parts += [cosine, -sine]
    return np.concatenate(parts, axis=0).astype(ml_dtypes.bfloat16)


def through(first, second, table):
    parts = []
    for values in (first, second):
        high = values.astype(jnp.bfloat16)
        parts += [high, (values - high.astype(jnp.float32)).astype(jnp.bfloat16)]
    count = first.shape[0]
    result = jnp.dot(jnp.concatenate(parts, axis=0), table, preferred_element_type=jnp.float32)
    blocks = [result[n * count : (n + 1) * count] for n in range(4)]
    return blocks[0] + blocks[1], blocks[2] + blocks[3]


def once(values):
    return values.astype(jnp.bfloat16).astype(jnp.float32)


def spectra_of(rows, forward_ref):
    normal = rows.astype(jnp.float32)
    count = rows.shape[0]
    rest = jnp.zeros((count, PLEN - rows.shape[1]), jnp.float32)
    quarters = [normal[:, n * QUARTER : (n + 1) * QUARTER] for n in range(3)]
    quarters.append(jnp.concatenate([normal[:, 3 * QUARTER :], rest], axis=1))
    sums = (quarters[0] + quarters[2], quarters[1] + quarters[3])
    total, change = through(sums[0] + sums[1], sums[0] - sums[1], forward_ref[:QUARTER])
    of_total = lax.broadcasted_iota(jnp.int32, (count, QUARTER), 1) < QUARTER // 2
    even = [jnp.where(of_total, total[:, half], change[:, half]) for half in (slice(0, QUARTER), slice(QUARTER, NF))]
    ahead, behind = through(quarters[0] - quarters[2], quarters[1] - quarters[3], forward_ref[QUARTER:])
    odd = [ahead[:, :QUARTER] + behind[:, QUARTER:], ahead[:, QUARTER:] - behind[:, :QUARTER]]
    return [once(part) for part in even + odd]


def doubled(part, window):
    rows = part[window * STEP : (window + 1) * STEP]
    return jnp.concatenate([rows, rows], axis=0)


def cross_and_back(right, left_ref, inverse_ref, out_ref):
    middle = lax.broadcasted_iota(jnp.int32, (8, QUARTER), 0) < STEP - 8

    def left_rows(window, pair, begin):
        picked = []
        for q in (2 * pair, 2 * pair + 1):
            row = window * STEP + q % COMP * STA + q // COMP
            picked.append(jnp.broadcast_to(left_ref[row : row + 1, begin : begin + QUARTER], (8, QUARTER)))
        return jnp.concatenate([picked[0], jnp.where(middle, picked[0], picked[1]), picked[1]], axis=0)

    columns = []
    for h in range(2):
        re, im = h * NF, h * NF + QUARTER
        right_re = [doubled(right[2 * h], w) for w in range(WIN)]
        right_im = [doubled(right[2 * h + 1], w) for w in range(WIN)]
        reals, imags = [], []
        for pair in range(STEP // 2):
            real, imag = 0.0, 0.0
            for w in range(WIN):
                left_re, left_im = left_rows(w, pair, re), left_rows(w, pair, im)
                real += left_re * right_re[w] + left_im * right_im[w]
                imag += left_re * right_im[w] - left_im * right_re[w]
            reals.append(real.astype(jnp.bfloat16))
            imags.append(imag.astype(jnp.bfloat16))
        columns += [jnp.concatenate(reals, axis=0), jnp.concatenate(imags, axis=0)]
    cross = jnp.concatenate(columns, axis=1)
    lags = jnp.dot(cross, inverse_ref[...], preferred_element_type=jnp.float32) * LAG_SCALE
    out_ref[...] = lags.astype(jnp.bfloat16).reshape(out_ref.shape)


def order_kernel(traces_ref, assign_ref, rows_ref, held, order, placed, sems):
    fetch_order = pltpu.make_async_copy(assign_ref, order, sems.at[STA])
    fetch_order.start()
    fetches = [pltpu.make_async_copy(traces_ref.at[r], held.at[r], sems.at[r]) for r in range(STA)]
    for fetch in fetches:
        fetch.start()
    last = LONG - 128
    placed[:, last:] = jnp.zeros((WIN * STEP, 128), jnp.float32)
    fetch_order.wait()
    for r in range(STA):
        fetches[r].wait()
        place = order[r]
        for j in range(COMP):
            both = held[r, j].astype(jnp.float32)
            for w in range(WIN):
                placed[pl.ds(w * STEP + j * STA + place, 1), :NSAMP] = both[w : w + 1]
    values = placed[...]
    energy = jnp.sum(values * values, axis=-1, keepdims=True) * (1.0 / NSAMP)
    rows_ref[...] = (values * lax.rsqrt(energy + EPSILON)).astype(jnp.bfloat16)


def own_kernel(rows_ref, *refs):
    sources, (left_ref, *targets), sems = refs[:3], refs[3:7], refs[7]
    fetches = [pltpu.make_async_copy(sources[n], targets[n], sems.at[n]) for n in range(3)]
    for fetch in fetches:
        fetch.start()
    fetches[0].wait()
    for n, part in enumerate(spectra_of(rows_ref[...], targets[0])):
        left_ref[:, n * QUARTER : (n + 1) * QUARTER] = part
    fetches[1].wait()
    fetches[2].wait()


def between_kernel(choose, rows_ref, left_ref, plan_ref, forward_ref, inverse_ref, out_ref):
    right = spectra_of(rows_ref[...], forward_ref)
    if choose:
        away = plan_ref[:, 0:1] != 0
        right = [jnp.where(away, part, left_ref[:, n * QUARTER : (n + 1) * QUARTER]) for n, part in enumerate(right)]
    cross_and_back(right, left_ref, inverse_ref, out_ref)


def within_kernel(rows_ref, left_ref, forward_ref, inverse_ref, between_ref, out_ref, between_out_ref):
    right = spectra_of(rows_ref[...], forward_ref)
    cross_and_back(right, left_ref, inverse_ref, out_ref)
    between_out_ref[...] = between_ref[...]


def in_vmem():
    return pl.BlockSpec(memory_space=pltpu.VMEM)


def in_hbm():
    return pl.BlockSpec(memory_space=pltpu.HBM)


OUT = jax.ShapeDtypeStruct((STA, COMP, COMP, STA, LAGS), jnp.bfloat16)


COST = pl.CostEstimate(flops=0, bytes_accessed=1000, transcendentals=0)


def params():
    return pltpu.CompilerParams(vmem_limit_bytes=24 * 2**20)


def order_rows(traces, assign):
    return pl.pallas_call(
        order_kernel,
        out_shape=jax.ShapeDtypeStruct((WIN * STEP, LONG), jnp.bfloat16),
        in_specs=[in_hbm(), in_hbm()],
        out_specs=in_vmem(),
        scratch_shapes=[
            pltpu.VMEM((STA, COMP, WIN, NSAMP), jnp.bfloat16),
            pltpu.SMEM((STA,), jnp.int32),
            pltpu.VMEM((WIN * STEP, LONG), jnp.float32),
            pltpu.SemaphoreType.DMA((STA + 1,)),
        ],
        compiler_params=params(),
        cost_estimate=COST,
    )(pltpu.with_memory_space_constraint(traces, pltpu.HBM), pltpu.with_memory_space_constraint(assign, pltpu.HBM))


def own_spectra(rows, *arrays):
    return pl.pallas_call(
        own_kernel,
        out_shape=[jax.ShapeDtypeStruct((WIN * STEP, 2 * NF), jnp.float32)]
        + [jax.ShapeDtypeStruct(array.shape, array.dtype) for array in arrays],
        in_specs=[in_vmem()] + [in_hbm()] * 3,
        out_specs=[in_vmem()] * 4,
        scratch_shapes=[pltpu.SemaphoreType.DMA((3,))],
        compiler_params=params(),
        cost_estimate=COST,
    )(rows, *(pltpu.with_memory_space_constraint(array, pltpu.HBM) for array in arrays))


def correlate_between(choose, rows, left, plan, forward, inverse):
    return pl.pallas_call(
        functools.partial(between_kernel, choose),
        out_shape=OUT,
        in_specs=[in_vmem()] * 5,
        out_specs=in_vmem(),
        compiler_params=params(),
        cost_estimate=COST,
    )(rows, left, plan, forward, inverse)


def correlate_within(rows, left, forward, inverse, between):
    return pl.pallas_call(
        within_kernel,
        out_shape=[OUT, OUT],
        in_specs=[in_vmem()] * 5,
        out_specs=[in_vmem(), in_vmem()],
        compiler_params=params(),
        cost_estimate=COST,
    )(rows, left, forward, inverse, between)


def shards(groups, blocks, traces, assign, matching):
    forward = jnp.asarray(np.concatenate([forward_table(EVEN_BINS), forward_table(ODD_BINS)], axis=0))
    inverse = jnp.asarray(inverse_table())
    long_rows = order_rows(traces, assign)
    beside = lax.ppermute(long_rows, "blk", [((i - 1) % blocks, i) for i in range(blocks)])
    other = long_rows[:, :NSAMP]
    bits = [1 << n for n in range((groups - 1).bit_length())]
    for bit in bits:
        swapped = lax.ppermute(other, "group", [(g ^ bit, g) for g in range(groups)])
        other = swapped if groups == 2 else jnp.where((matching[0, 0] & bit) != 0, swapped, other)
    left, forward, inverse, plan = own_spectra(long_rows, forward, inverse, matching)
    between = correlate_between(groups == 2, other, left, plan, forward, inverse)
    within, between = correlate_within(beside, left, forward, inverse, between)
    return (between.transpose(0, 3, 1, 2, 4), within.transpose(0, 3, 1, 2, 4))


def solution(mesh):
    placed = (P(("group", "blk"), None, None, None), P(("group", "blk")), P("blk", None))
    return jax.shard_map(
        functools.partial(shards, mesh.shape["group"], mesh.shape["blk"]),
        mesh=mesh,
        in_specs=placed,
        out_specs=(
            P(("group", "blk"), None, None, None, None),
            P(("group", "blk"), None, None, None, None),
        ),
        check_vma=False,
    )
```

```python
import functools
import math

import jax
import jax.numpy as jnp
import ml_dtypes
import numpy as np
from jax import lax
from jax.experimental import pallas as pl
from jax.experimental.pallas import tpu as pltpu
from jax.sharding import PartitionSpec as P

STA = 4
COMP = 3
WIN = 2
NSAMP = 1200
PLEN = 1536
NF = 768
QUARTER = PLEN // 4
HALF = 200
LAGS = 401
STEP = COMP * STA
LONG = 1280

EPSILON = 1e-05
LAG_SCALE = 2.0 / (PLEN * math.sqrt(NSAMP * WIN))

EVEN_BINS = np.concatenate([np.arange(4, NF + 1, 4), np.arange(2, NF + 1, 4)])
ODD_BINS = np.arange(1, PLEN, 4)


def turned(ids_a, ids_b):
    phases = ids_a[:, None] * ids_b[None, :] % PLEN * (2.0 * math.pi / PLEN)
    return np.cos(phases), np.sin(phases)


def forward_table(bins):
    cosine, sine = turned(np.arange(QUARTER), bins)
    return np.concatenate([cosine, -sine], axis=1).astype(ml_dtypes.bfloat16)


def inverse_table():
    lags = np.arange(LAGS) - HALF
    parts = []
    for bins in (EVEN_BINS, ODD_BINS):
        cosine, sine = turned(bins, lags)
        parts += [cosine, -sine]
    return np.concatenate(parts, axis=0).astype(ml_dtypes.bfloat16)


def once(values):
    return values.astype(jnp.bfloat16).astype(jnp.float32)


def spectra_of(rows, forward_ref):
    samples = rows.astype(jnp.float32)
    count = rows.shape[0]
    rest = jnp.zeros((count, PLEN - rows.shape[1]), jnp.float32)
    quarters = [samples[:, n * QUARTER : (n + 1) * QUARTER] for n in range(3)]
    quarters.append(jnp.concatenate([samples[:, 3 * QUARTER :], rest], axis=1))
    stacked = jnp.concatenate(quarters, axis=0).astype(jnp.bfloat16)
    result = jnp.dot(stacked, forward_ref[...], preferred_element_type=jnp.float32)
    parts = [result[n * count : (n + 1) * count] for n in range(4)]
    evens, odds = [part[:, :NF] for part in parts], [part[:, NF:] for part in parts]
    same, other = evens[0] + evens[2], evens[1] + evens[3]
    added = lax.broadcasted_iota(jnp.int32, (count, QUARTER), 1) < QUARTER // 2
    even = [same[:, half] + jnp.where(added, other[:, half], -other[:, half]) for half in (slice(0, QUARTER), slice(QUARTER, NF))]
    ahead, behind = odds[0] - odds[2], odds[1] - odds[3]
    odd = [ahead[:, :QUARTER] + behind[:, QUARTER:], ahead[:, QUARTER:] - behind[:, :QUARTER]]
    return [once(part) for part in even + odd]


def doubled(part, window):
    rows = part[window * STEP : (window + 1) * STEP]
    return jnp.concatenate([rows, rows], axis=0)


def cross_and_back(right, left_ref, inverse_ref, out_ref):
    middle = lax.broadcasted_iota(jnp.int32, (8, QUARTER), 0) < STEP - 8

    def left_rows(window, pair, begin):
        picked = []
        for q in (2 * pair, 2 * pair + 1):
            row = window * STEP + q % COMP * STA + q // COMP
            picked.append(jnp.broadcast_to(left_ref[row : row + 1, begin : begin + QUARTER], (8, QUARTER)))
        return jnp.concatenate([picked[0], jnp.where(middle, picked[0], picked[1]), picked[1]], axis=0)

    columns = []
    for h in range(2):
        re, im = h * NF, h * NF + QUARTER
        right_re = [doubled(right[2 * h], w) for w in range(WIN)]
        right_im = [doubled(right[2 * h + 1], w) for w in range(WIN)]
        reals, imags = [], []
        for pair in range(STEP // 2):
            real, imag = 0.0, 0.0
            for w in range(WIN):
                left_re, left_im = left_rows(w, pair, re), left_rows(w, pair, im)
                real += left_re * right_re[w] + left_im * right_im[w]
                imag += left_re * right_im[w] - left_im * right_re[w]
            reals.append(real.astype(jnp.bfloat16))
            imags.append(imag.astype(jnp.bfloat16))
        columns += [jnp.concatenate(reals, axis=0), jnp.concatenate(imags, axis=0)]
    cross = jnp.concatenate(columns, axis=1)
    lags = jnp.dot(cross, inverse_ref[...], preferred_element_type=jnp.float32) * LAG_SCALE
    out_ref[...] = lags.astype(jnp.bfloat16).reshape(out_ref.shape)


def order_kernel(traces_ref, assign_ref, rows_ref, held, order, placed, sems):
    fetch_order = pltpu.make_async_copy(assign_ref, order, sems.at[STA])
    fetch_order.start()
    fetches = [pltpu.make_async_copy(traces_ref.at[r], held.at[r], sems.at[r]) for r in range(STA)]
    for fetch in fetches:
        fetch.start()
    last = LONG - 128
    placed[:, last:] = jnp.zeros((WIN * STEP, 128), jnp.float32)
    fetch_order.wait()
    for r in range(STA):
        fetches[r].wait()
        place = order[r]
        for j in range(COMP):
            both = held[r, j].astype(jnp.float32)
            for w in range(WIN):
                placed[pl.ds(w * STEP + j * STA + place, 1), :NSAMP] = both[w : w + 1]
    values = placed[...]
    energy = jnp.sum(values * values, axis=-1, keepdims=True) * (1.0 / NSAMP)
    rows_ref[...] = (values * lax.rsqrt(energy + EPSILON)).astype(jnp.bfloat16)


def own_kernel(rows_ref, *refs):
    sources, (left_ref, *targets), sems = refs[:3], refs[3:7], refs[7]
    fetches = [pltpu.make_async_copy(sources[n], targets[n], sems.at[n]) for n in range(3)]
    for fetch in fetches:
        fetch.start()
    fetches[0].wait()
    for n, part in enumerate(spectra_of(rows_ref[...], targets[0])):
        left_ref[:, n * QUARTER : (n + 1) * QUARTER] = part
    fetches[1].wait()
    fetches[2].wait()


def between_kernel(choose, rows_ref, left_ref, plan_ref, forward_ref, inverse_ref, out_ref):
    right = spectra_of(rows_ref[...], forward_ref)
    if choose:
        away = plan_ref[:, 0:1] != 0
        right = [jnp.where(away, part, left_ref[:, n * QUARTER : (n + 1) * QUARTER]) for n, part in enumerate(right)]
    cross_and_back(right, left_ref, inverse_ref, out_ref)


def within_kernel(rows_ref, left_ref, forward_ref, inverse_ref, between_ref, out_ref, between_out_ref):
    right = spectra_of(rows_ref[...], forward_ref)
    cross_and_back(right, left_ref, inverse_ref, out_ref)
    between_out_ref[...] = between_ref[...]


def in_vmem():
    return pl.BlockSpec(memory_space=pltpu.VMEM)


def in_hbm():
    return pl.BlockSpec(memory_space=pltpu.HBM)


OUT = jax.ShapeDtypeStruct((STA, COMP, COMP, STA, LAGS), jnp.bfloat16)


COST = pl.CostEstimate(flops=0, bytes_accessed=1000, transcendentals=0)


def params():
    return pltpu.CompilerParams(vmem_limit_bytes=24 * 2**20)


def order_rows(traces, assign):
    return pl.pallas_call(
        order_kernel,
        out_shape=jax.ShapeDtypeStruct((WIN * STEP, LONG), jnp.bfloat16),
        in_specs=[in_hbm(), in_hbm()],
        out_specs=in_vmem(),
        scratch_shapes=[
            pltpu.VMEM((STA, COMP, WIN, NSAMP), jnp.bfloat16),
            pltpu.SMEM((STA,), jnp.int32),
            pltpu.VMEM((WIN * STEP, LONG), jnp.float32),
            pltpu.SemaphoreType.DMA((STA + 1,)),
        ],
        compiler_params=params(),
        cost_estimate=COST,
    )(pltpu.with_memory_space_constraint(traces, pltpu.HBM), pltpu.with_memory_space_constraint(assign, pltpu.HBM))


def own_spectra(rows, *arrays):
    return pl.pallas_call(
        own_kernel,
        out_shape=[jax.ShapeDtypeStruct((WIN * STEP, 2 * NF), jnp.float32)]
        + [jax.ShapeDtypeStruct(array.shape, array.dtype) for array in arrays],
        in_specs=[in_vmem()] + [in_hbm()] * 3,
        out_specs=[in_vmem()] * 4,
        scratch_shapes=[pltpu.SemaphoreType.DMA((3,))],
        compiler_params=params(),
        cost_estimate=COST,
    )(rows, *(pltpu.with_memory_space_constraint(array, pltpu.HBM) for array in arrays))


def correlate_between(choose, rows, left, plan, forward, inverse):
    return pl.pallas_call(
        functools.partial(between_kernel, choose),
        out_shape=OUT,
        in_specs=[in_vmem()] * 5,
        out_specs=in_vmem(),
        compiler_params=params(),
        cost_estimate=COST,
    )(rows, left, plan, forward, inverse)


def correlate_within(rows, left, forward, inverse, between):
    return pl.pallas_call(
        within_kernel,
        out_shape=[OUT, OUT],
        in_specs=[in_vmem()] * 5,
        out_specs=[in_vmem(), in_vmem()],
        compiler_params=params(),
        cost_estimate=COST,
    )(rows, left, forward, inverse, between)


def shards(groups, blocks, traces, assign, matching):
    forward = jnp.asarray(np.concatenate([forward_table(EVEN_BINS), forward_table(ODD_BINS)], axis=1))
    inverse = jnp.asarray(inverse_table())
    long_rows = order_rows(traces, assign)
    beside = lax.ppermute(long_rows, "blk", [((i - 1) % blocks, i) for i in range(blocks)])
    other = long_rows[:, :NSAMP]
    bits = [1 << n for n in range((groups - 1).bit_length())]
    for bit in bits:
        swapped = lax.ppermute(other, "group", [(g ^ bit, g) for g in range(groups)])
        other = swapped if groups == 2 else jnp.where((matching[0, 0] & bit) != 0, swapped, other)
    left, forward, inverse, plan = own_spectra(long_rows, forward, inverse, matching)
    between = correlate_between(groups == 2, other, left, plan, forward, inverse)
    within, between = correlate_within(beside, left, forward, inverse, between)
    return (between.transpose(0, 3, 1, 2, 4), within.transpose(0, 3, 1, 2, 4))


def solution(mesh):
    placed = (P(("group", "blk"), None, None, None), P(("group", "blk")), P("blk", None))
    return jax.shard_map(
        functools.partial(shards, mesh.shape["group"], mesh.shape["blk"]),
        mesh=mesh,
        in_specs=placed,
        out_specs=(
            P(("group", "blk"), None, None, None, None),
            P(("group", "blk"), None, None, None, None),
        ),
        check_vma=False,
    )
```
